32 devices in a mesh: ctx: 8 (over z, y), head: 4 (over x, core).
Axes of the slice: x: 2, y: 2, z: 4, core: 2. Of those that a mesh axis runs over, the one named last changes fastest.
Arguments:
- hidden: bfloat16 [2048, 2560], P('ctx'), may hold values from -6 to 6
- norm_gain: float32 [2560], replicated, may hold values from 0.1 to 1.9
- x_weight: bfloat16 [2560, 5120], P(None, 'head'), may hold values from -0.125 to 0.125
- z_weight: bfloat16 [2560, 5120], P(None, 'head'), may hold values from -0.125 to 0.125
- bc_weight: bfloat16 [2560, 256], replicated, may hold values from -0.125 to 0.125
- dt_weight: bfloat16 [2560, 80], P(None, 'head'), may hold values from -0.125 to 0.125
- x_kernel: float32 [4, 5120], P(None, 'head'), may hold values from -3 to 3
- bc_kernel: float32 [4, 256], replicated, may hold values from -3 to 3
- dt_bias: float32 [80], P('head'), may hold values from -1 to 1
- log_rate: float32 [80], P('head'), may hold values from -13 to -3
- out_gain: float32 [5120], P('head'), may hold values from 0.1 to 1.9
- out_weight: bfloat16 [5120, 2560], P('head'), may hold values from -0.078125 to 0.078125
Outputs:
- layer_out: bfloat16 [2048, 2560], P('ctx', 'head')
The draws below stay inside these ranges and needn't reach their ends.
All inputs are finite; a program needn't handle non-finite values.
Results may differ from the reference program's by a relative error of at most 0.014.
Values may be sent and summed in bfloat16 or wider, within the bound.
A program may use at most 128 MiB of HBM per device.

```python
import jax
import jax.numpy as jnp
from jax import lax

D = 2560
HEADS = 80
HEAD_DIM = 64
STATE = 128
CONV = 4
L_DEV = 256
INNER = 5120
TOKENS = 2048


def draw_log_rate(key, part):
    order_key = jax.random.fold_in(key, 11)
    slow_key = jax.random.fold_in(key, 12)
    fast_key = jax.random.fold_in(key, 13)
    slow_count = HEADS // 2
    rank_order = jax.random.permutation(order_key, HEADS)
    slow_heads = rank_order < slow_count
    slow_rate = jnp.log(0.2 / TOKENS) + jnp.log(5.0) * jax.random.uniform(slow_key, (HEADS,), jnp.float32)
    fast_rate = jnp.log(1.0 / 50.0) + jnp.log(50.0 / 30.0) * jax.random.uniform(fast_key, (HEADS,), jnp.float32)
    return jnp.where(slow_heads, slow_rate, fast_rate).astype(jnp.float32)


def steps_of(rng, extent, cuts, smallest, top_value):
    level, own = 1.0, jax.random.fold_in(rng, 6)
    for dim, shards_of in cuts:
        heights = jnp.exp(jax.random.uniform(jax.random.fold_in(own, dim), (shards_of,), jnp.float32, smallest / len(cuts), top_value / len(cuts)))
        level = level * jnp.repeat(heights, extent[dim] // shards_of).reshape([-1 if axis == dim else 1 for axis in range(len(extent))])
    return level


def gaussian(stream_key, extent, spread, reach, cuts=(), held_as=jnp.bfloat16):
    gain = steps_of(stream_key, extent, cuts, -0.22, 0.18) if cuts else 1.0
    values = jax.random.normal(stream_key, extent, jnp.float32) * spread * gain
    return jnp.minimum(jnp.maximum(values, -reach), reach).astype(held_as)


def setup_inputs(seed: int = 0) -> dict:
    streams_of = jax.random.split(jax.random.key(seed), 13)
    hidden = gaussian(streams_of[0], (TOKENS, D), 1.0, 6.0, ((0, 8),))
    norm_gain = jnp.clip(1.0 + 0.18 * jax.random.normal(streams_of[1], (D,), jnp.float32), 0.1, 1.9)
    x_weight = gaussian(streams_of[2], (D, INNER), D ** -0.5, 0.125, ((1, 4),))
    z_weight = gaussian(streams_of[3], (D, INNER), D ** -0.5, 0.125, ((1, 4),))
    bc_weight = gaussian(streams_of[4], (D, 2 * STATE), D ** -0.5, 0.125)
    dt_weight = gaussian(streams_of[5], (D, HEADS), D ** -0.5, 0.125, ((1, 4),))
    x_kernel = gaussian(streams_of[6], (CONV, INNER), 0.5, 3.0, ((1, 4),), jnp.float32)
    bc_kernel = gaussian(streams_of[7], (CONV, 2 * STATE), 0.5, 3.0, (), jnp.float32)
    dt_bias = jnp.clip(jax.random.uniform(streams_of[8], (HEADS,), jnp.float32, -1.0, 1.0) * steps_of(streams_of[8], (HEADS,), ((0, 4),), -0.4, 0.0), -1.0, 1.0)
    log_rate = draw_log_rate(jax.random.fold_in(streams_of[12], 71), 0)
    out_gain = jnp.clip(1.0 + 0.18 * jax.random.normal(streams_of[10], (INNER,), jnp.float32), 0.1, 1.9)
    out_weight = gaussian(streams_of[11], (INNER, D), INNER ** -0.5, 0.078125, ((0, 4),))
    return {"hidden": hidden, "norm_gain": norm_gain, "x_weight": x_weight, "z_weight": z_weight, "bc_weight": bc_weight, "dt_weight": dt_weight, "x_kernel": x_kernel, "bc_kernel": bc_kernel, "dt_bias": dt_bias, "log_rate": log_rate, "out_gain": out_gain, "out_weight": out_weight}


epsilon = 1e-05
highest = lax.Precision.HIGHEST

def rms_scale(values, scaling):
    mean_sq = lax.optimization_barrier(jnp.mean(values * values, axis=-1, keepdims=True))
    return values * lax.rsqrt(mean_sq + epsilon) * scaling

def conv_silu(series, kernel):
    tap_count = kernel.shape[0]
    row_count = series.shape[0]
    padded = jnp.concatenate([jnp.zeros((tap_count - 1, series.shape[1]), series.dtype), series], axis=0)
    running = jnp.zeros(series.shape, jnp.float32)
    for offset in range(tap_count):
        running = running + kernel[offset] * padded[offset:offset + row_count].astype(jnp.float32)
    return jax.nn.silu(running).astype(jnp.bfloat16)

def block_scan(carried, pieces):
    x_blk, b_blk, c_blk, step_blk, decay_blk = pieces
    row_count = x_blk.shape[0]
    cumulative = jnp.cumsum(decay_blk, axis=0)
    cumul_heads = cumulative.T
    step_heads = step_blk.T
    gram_rows = jnp.dot(c_blk, b_blk.T, preferred_element_type=jnp.float32)
    causal = jnp.arange(row_count)[:, None] >= jnp.arange(row_count)[None, :]
    segment = cumul_heads[:, :, None] - cumul_heads[:, None, :]
    weights = jnp.exp(jnp.where(causal[None], segment, -jnp.inf)) * gram_rows[None] * step_heads[:, None, :]
    x_float = x_blk.astype(jnp.float32)
    b_float = b_blk.astype(jnp.float32)
    c_float = c_blk.astype(jnp.float32)
    within = jnp.einsum('hts,shp->thp', weights, x_float, precision=highest)
    from_carry = jnp.einsum('tn,hpn->thp', c_float, carried, precision=highest) * jnp.exp(cumulative)[:, :, None]
    final_log = cumul_heads[:, -1]
    weight_end = jnp.exp(final_log[:, None] - cumul_heads) * step_heads
    local_state = jnp.einsum('hs,shp,sn->hpn', weight_end, x_float, b_float, precision=highest)
    new_carry = jnp.exp(final_log)[:, None, None] * carried + local_state
    y_full = within + from_carry
    return (new_carry, y_full)

def mixer(stream, params):
    norm_gain, x_weight, z_weight, bc_weight, dt_weight, x_kernel, bc_kernel, dt_bias, log_rate, out_gain = params
    row_count = stream.shape[0]
    normed = rms_scale(stream.astype(jnp.float32), norm_gain).astype(jnp.bfloat16)
    x_in = jnp.dot(normed, x_weight, preferred_element_type=jnp.float32).astype(jnp.bfloat16)
    z_in = jnp.dot(normed, z_weight, preferred_element_type=jnp.float32).astype(jnp.bfloat16)
    bc_in = jnp.dot(normed, bc_weight, preferred_element_type=jnp.float32).astype(jnp.bfloat16)
    dt_raw = jnp.dot(normed, dt_weight, preferred_element_type=jnp.float32)
    x_conv = conv_silu(x_in, x_kernel)
    bc_conv = conv_silu(bc_in, bc_kernel)
    step_size = jax.nn.softplus(dt_raw + dt_bias)
    log_decay = -step_size * jnp.exp(log_rate)
    blocks = row_count // L_DEV
    pieces = (x_conv.reshape(blocks, L_DEV, HEADS, HEAD_DIM), bc_conv[:, :STATE].reshape(blocks, L_DEV, STATE), bc_conv[:, STATE:].reshape(blocks, L_DEV, STATE), step_size.reshape(blocks, L_DEV, HEADS), log_decay.reshape(blocks, L_DEV, HEADS))
    initial = jnp.zeros((HEADS, HEAD_DIM, STATE), jnp.float32)
    carried, y_blocks = lax.scan(block_scan, initial, pieces)
    y_full = y_blocks.reshape(row_count, HEADS, HEAD_DIM)
    gating = jax.nn.silu(z_in.astype(jnp.float32)).reshape(row_count, HEADS, HEAD_DIM)
    gated_out = rms_scale(y_full * gating, out_gain.reshape(HEADS, HEAD_DIM))
    return gated_out.astype(jnp.bfloat16).reshape(row_count, HEADS * HEAD_DIM)

def reference(hidden, norm_gain, x_weight, z_weight, bc_weight, dt_weight, x_kernel, bc_kernel, dt_bias, log_rate, out_gain, out_weight):
    params = (norm_gain, x_weight, z_weight, bc_weight, dt_weight, x_kernel, bc_kernel, dt_bias, log_rate, out_gain)
    h_rows = hidden
    h_rc = h_rows[::-1, ::-1]
    forward_out = jnp.dot(mixer(h_rows, params), out_weight, preferred_element_type=jnp.float32)
    backward_out = jnp.dot(mixer(h_rc, params), out_weight, preferred_element_type=jnp.float32)[::-1, ::-1]
    return (h_rows.astype(jnp.float32) + (forward_out + backward_out)).astype(jnp.bfloat16)
```

```python
import functools

import jax
import jax.numpy as jnp
from jax import lax
from jax.experimental import pallas as pl
from jax.experimental.pallas import tpu as pltpu
from jax.sharding import PartitionSpec as P

HEAD_DIM = 64
STATE = 128
GROUP = 256
LANES = 128
HALO = 16
epsilon = 1e-05
highest = lax.Precision.HIGHEST
MESH = pl.DeviceIdType.MESH
f32 = jnp.float32
bf16 = jnp.bfloat16


def iota(shape, dim):
    return lax.broadcasted_iota(jnp.int32, shape, dim)


def dot(a, b, precision=None):
    return jnp.dot(a, b, preferred_element_type=f32, precision=precision)


def silu(v):
    return v / (1.0 + jnp.exp(-v))


def anti(size):
    return (iota((size, size), 0) + iota((size, size), 1) == size - 1).astype(bf16)


def spread(group):
    head = group * (GROUP // HEAD_DIM) + iota((LANES, GROUP), 1) // HEAD_DIM
    return (iota((LANES, GROUP), 0) == head).astype(f32)


def conv_fwd(ext, taps, rows):
    out = taps[0:1] * ext[HALO - 3 : HALO - 3 + rows]
    for k in range(1, 4):
        out = out + taps[k : k + 1] * ext[HALO - 3 + k : HALO - 3 + k + rows]
    return silu(out).astype(bf16)


def conv_bwd(ext, taps, rows):
    out = taps[0:1] * ext[3 : 3 + rows]
    for k in range(1, 4):
        out = out + taps[k : k + 1] * ext[3 - k : 3 - k + rows]
    return silu(out).astype(bf16)


def first_kernel(
    h_ref, prev_ref, next_ref, gain_ref, bcw_ref, dtw_ref, bck_ref, dtb_ref, rate_ref, xw_ref, xk_ref,
    n_ref, bc_ref, delta_ref, cum_ref, cumt_ref, x_ref, s_ref, dec_ref,
    next_n, wend, pad,
):
    rows, width = h_ref.shape
    ext = rows + HALO
    group = pl.program_id(0)

    @pl.when(group == 0)
    def _():
        gain = gain_ref[...]
        blocks = width // GROUP
        flip = anti(GROUP)

        def turned(ref):
            parts = [
                dot(ref[:, (blocks - 1 - j) * GROUP : (blocks - j) * GROUP], flip) for j in range(blocks)
            ]
            return jnp.concatenate(parts, axis=1)

        def scale(u):
            return lax.rsqrt(jnp.mean(u * u, axis=1, keepdims=True) + epsilon)

        here = h_ref[...].astype(f32)
        factor = scale(here)
        n_ref[HALO:ext, :] = (here * factor * gain).astype(bf16)
        n_ref[ext : ext + rows, :] = (turned(h_ref) * factor * gain).astype(bf16)
        prior = prev_ref[...].astype(f32)
        n_ref[0:HALO, :] = (prior * scale(prior) * gain).astype(bf16)
        later = turned(next_ref)
        n_ref[ext + rows :, :] = (later * scale(later) * gain).astype(bf16)

        bc_in = dot(n_ref[...], bcw_ref[...]).astype(bf16).astype(f32)
        bc_ref[0] = conv_fwd(bc_in[:ext], bck_ref[...], rows)
        bc_ref[1] = conv_bwd(bc_in[ext:], bck_ref[...], rows)

        raw = dot(n_ref[HALO : ext + rows, :], dtw_ref[...]) + dtb_ref[...]
        step = jnp.maximum(raw, 0.0) + jnp.log1p(jnp.exp(-jnp.abs(raw)))
        decay = -step * jnp.exp(rate_ref[...])
        heads = raw.shape[1]
        pad[...] = jnp.zeros_like(pad)
        pad[0, :, 0:heads] = step
        pad[1, :, 0:heads] = decay
        tri = iota((rows, rows), 0) >= iota((rows, rows), 1)
        for d in range(2):
            mine = slice(d * rows, (d + 1) * rows)
            mask = tri if d == 0 else iota((rows, rows), 0) <= iota((rows, rows), 1)
            cum = dot(mask.astype(f32), pad[1, mine, :], highest)
            end = cum[rows - 1 : rows] if d == 0 else cum[0:1]
            delta_ref[d] = pad[0, mine, :]
            cum_ref[d] = cum
            cumt_ref[d] = cum.T
            wend[d] = jnp.exp(end - cum) * pad[0, mine, :]
            next_n[d] = jnp.broadcast_to(jnp.exp(end), (8, LANES))

    x_in = dot(n_ref[...], xw_ref[...]).astype(bf16).astype(f32)
    taps = xk_ref[...]
    hot = spread(group)
    for d in range(2):
        x_conv = conv_fwd(x_in[:ext], taps, rows) if d == 0 else conv_bwd(x_in[ext:], taps, rows)
        x_ref[d, 0] = x_conv
        weighted = (x_conv.astype(f32) * dot(wend[d], hot, highest)).astype(bf16)
        s_ref[d, 0] = lax.dot_general(
            bc_ref[d, :, :STATE], weighted, (((0,), (0,)), ((), ())), preferred_element_type=f32
        ).astype(bf16)
        dec_ref[d, 0] = dot(next_n[d], hot, highest)


def second_kernel(
    n_ctx, axes,
    n_ref, bc_ref, delta_ref, cum_ref, cumt_ref, x_ref, s_ref, dec_ref, gain_ref, h_ref, zw_hbm, ow_hbm,
    out_ref,
    zw, ow, z_buf, y_buf, gated, gram, carry, send_buf, one_send, one_recv, two_send, two_recv,
    zw_sem, ow_sem, c_send, c_recv, r_send, r_recv,
):
    ctx_axis, head_axis = axes
    me = lax.axis_index(ctx_axis)
    place = lax.axis_index(head_axis)
    groups = x_ref.shape[1]
    rows = x_ref.shape[2]
    block = out_ref.shape[1]
    core = lax.rem(place, 2)
    side = place // 2
    sibling = side * 2 + (1 - core)
    across = (1 - side) * 2 + core

    z_copies = [
        pltpu.make_async_copy(zw_hbm.at[:, pl.ds(g * GROUP, GROUP)], zw.at[g], zw_sem.at[g])
        for g in range(groups)
    ]
    o_copy = pltpu.make_async_copy(ow_hbm, ow, ow_sem)
    for copy in z_copies:
        copy.start()
    o_copy.start()

    barrier = pltpu.get_barrier_semaphore()
    for peer in (sibling, across):
        pl.semaphore_signal(barrier, inc=1, device_id={head_axis: peer}, device_id_type=MESH)

    @pl.when(me > 0)
    def _():
        pl.semaphore_signal(barrier, inc=1, device_id={ctx_axis: me - 1}, device_id_type=MESH)

    @pl.when(me < n_ctx - 1)
    def _():
        pl.semaphore_signal(barrier, inc=1, device_id={ctx_axis: me + 1}, device_id_type=MESH)

    ends = jnp.where(me > 0, 1, 0) + jnp.where(me < n_ctx - 1, 1, 0)
    pl.semaphore_wait(barrier, 2 + ends)

    def chain_copy(d, g, target):
        return pltpu.make_async_remote_copy(
            src_ref=send_buf.at[d, g],
            dst_ref=carry.at[d, g],
            send_sem=c_send.at[d, g],
            recv_sem=c_recv.at[d, g],
            device_id={ctx_axis: target},
            device_id_type=MESH,
        )

    def chain(d):
        target = me + 1 - 2 * d
        source = me - 1 + 2 * d
        has_source = jnp.logical_and(source >= 0, source < n_ctx)
        has_target = jnp.logical_and(target >= 0, target < n_ctx)

        def one(g, _):
            @pl.when(has_source)
            def _():
                chain_copy(d, g, source).wait_recv()

            @pl.when(jnp.logical_not(has_source))
            def _():
                carry[d, g] = jnp.zeros_like(carry[d, g])

            @pl.when(has_target)
            def _():
                total = carry[d, g].astype(f32) * dec_ref[d, g, 0:1, :] + s_ref[d, g].astype(f32)
                send_buf[d, g] = total.astype(bf16)
                chain_copy(d, g, target).start()

            return 0

        lax.fori_loop(0, groups, one, 0)

    def unit(g, _):
        pltpu.make_async_copy(zw_hbm.at[:, pl.ds(0, GROUP)], zw.at[g], zw_sem.at[g]).wait()
        z_buf[g] = dot(n_ref[HALO : HALO + 2 * rows, :], zw[g]).astype(bf16)
        hot = spread(g)
        lane_head = iota((rows, GROUP), 1) // HEAD_DIM
        for d in range(2):
            scaled = x_ref[d, g].astype(f32) * dot(delta_ref[d], hot, highest)
            cols = dot(cum_ref[d], hot, highest)
            parts, values = [], []
            for j in range(GROUP // HEAD_DIM):
                column = cols[:, j * HEAD_DIM : j * HEAD_DIM + 1]
                row = cumt_ref[d, pl.ds(g * (GROUP // HEAD_DIM) + j, 1), :]
                parts.append((jnp.exp(jnp.minimum(column - row, 0.0)) * gram[d]).astype(bf16))
                values.append(jnp.where(lane_head == j, scaled, 0.0).astype(bf16))
            y_buf[g, d] = dot(jnp.concatenate(parts, axis=1), jnp.concatenate(values, axis=0))
        return 0

    late = me >= n_ctx // 2
    first = jnp.where(late, 1, 0)
    distance = jnp.where(late, n_ctx - 1 - me, me)
    before = jnp.minimum(groups, distance + distance // 2)

    for d in range(2):
        full = lax.dot_general(
            bc_ref[d, :, STATE:], bc_ref[d, :, :STATE], (((1,), (1,)), ((), ())), preferred_element_type=f32
        )
        ahead = iota((rows, rows), 0) - iota((rows, rows), 1)
        gram[d] = jnp.where(ahead >= 0 if d == 0 else ahead <= 0, full, 0.0)

    lax.fori_loop(0, before, unit, 0)
    chain(first)
    lax.fori_loop(before, groups, unit, 0)
    chain(1 - first)

    same = iota((GROUP, GROUP), 0) // HEAD_DIM == iota((GROUP, GROUP), 1) // HEAD_DIM
    average = jnp.where(same, 1.0 / HEAD_DIM, 0.0).astype(bf16)
    growth = [jnp.exp(cum_ref[d]) for d in range(2)]
    for g in range(groups):
        hot = spread(g)
        for d in range(2):
            carried = dot(bc_ref[d, :, STATE:], carry[d, g]) * dot(growth[d], hot, highest)
            value = (y_buf[g, d] + carried) * silu(z_buf[g, d * rows : (d + 1) * rows].astype(f32))
            square = value * value
            high = square.astype(bf16)
            low = (square - high.astype(f32)).astype(bf16)
            mean_sq = dot(high, average) + dot(low, average)
            lanes = slice(g * GROUP, (g + 1) * GROUP)
            gated[d, :, lanes] = (
                value * lax.rsqrt(mean_sq + epsilon) * gain_ref[:, lanes]
            ).astype(bf16)

    o_copy.wait()
    flip = anti(LANES)
    blocks = ow_hbm.shape[1] // block

    def project(which):
        mine = pl.multiple_of(which * block, LANES)
        other = pl.multiple_of((blocks - 1 - which) * block, LANES)
        ahead = dot(gated[0], ow[:, pl.ds(mine, block)])
        back = dot(gated[1], ow[:, pl.ds(other, block)]).astype(bf16)
        count = block // LANES
        turned = [
            dot(back[:, (count - 1 - j) * LANES : (count - j) * LANES], flip) for j in range(count)
        ]
        return ahead + jnp.concatenate(turned, axis=1)

    def near(slot):
        return pltpu.make_async_remote_copy(
            src_ref=one_send.at[slot],
            dst_ref=one_recv.at[slot],
            send_sem=r_send.at[slot],
            recv_sem=r_recv.at[slot],
            device_id={head_axis: sibling},
            device_id_type=MESH,
        )

    far = pltpu.make_async_remote_copy(
        src_ref=two_send,
        dst_ref=two_recv,
        send_sem=r_send.at[2],
        recv_sem=r_recv.at[2],
        device_id={head_axis: across},
        device_id_type=MESH,
    )
    one_send[0] = project((1 - side) * 2 + (1 - core)).astype(bf16)
    near(0).start()
    partial = project(across)
    near(0).wait_recv()
    two_send[...] = (partial + one_recv[0].astype(f32)).astype(bf16)
    far.start()
    one_send[1] = project(sibling).astype(bf16)
    near(1).start()
    partial = project(place)
    residual = h_ref[:, pl.ds(pl.multiple_of(place * block, LANES), block)].astype(f32)
    near(1).wait_recv()
    partial = partial + one_recv[1].astype(f32)
    far.wait_recv()
    out_ref[...] = (residual + (partial + two_recv[...].astype(f32))).astype(out_ref.dtype)
    near(0).wait_send()
    near(1).wait_send()
    far.wait_send()

    def drain(g, _):
        @pl.when(me < n_ctx - 1)
        def _():
            chain_copy(0, g, me + 1).wait_send()

        @pl.when(me > 0)
        def _():
            chain_copy(1, g, me - 1).wait_send()

        return 0

    lax.fori_loop(0, groups, drain, 0)


def per_device(
    mesh,
    hidden,
    norm_gain,
    x_weight,
    z_weight,
    bc_weight,
    dt_weight,
    x_kernel,
    bc_kernel,
    dt_bias,
    log_rate,
    out_gain,
    out_weight,
):
    n_ctx = mesh.shape["ctx"]
    n_head = mesh.shape["head"]
    rows, width = hidden.shape
    inner = x_weight.shape[1]
    groups = inner // GROUP
    heads = inner // HEAD_DIM
    prev = lax.ppermute(hidden[rows - HALO :], "ctx", [(i, i + 1) for i in range(n_ctx - 1)])
    follow = lax.ppermute(hidden[:HALO], "ctx", [(i + 1, i) for i in range(n_ctx - 1)])

    def whole(*shape):
        return pl.BlockSpec(shape, lambda g: (0,) * len(shape))

    long = 2 * (rows + HALO)
    shapes = [
        jax.ShapeDtypeStruct((long, width), bf16),
        jax.ShapeDtypeStruct((2, rows, 2 * STATE), bf16),
        jax.ShapeDtypeStruct((2, rows, LANES), f32),
        jax.ShapeDtypeStruct((2, rows, LANES), f32),
        jax.ShapeDtypeStruct((2, LANES, rows), f32),
        jax.ShapeDtypeStruct((2, groups, rows, GROUP), bf16),
        jax.ShapeDtypeStruct((2, groups, STATE, GROUP), bf16),
        jax.ShapeDtypeStruct((2, groups, 8, GROUP), f32),
    ]
    made = pl.pallas_call(
        first_kernel,
        grid=(groups,),
        out_shape=shapes,
        in_specs=[
            whole(rows, width),
            whole(HALO, width),
            whole(HALO, width),
            whole(1, width),
            whole(width, 2 * STATE),
            whole(width, heads),
            whole(4, 2 * STATE),
            whole(1, heads),
            whole(1, heads),
            pl.BlockSpec((width, GROUP), lambda g: (0, g)),
            pl.BlockSpec((4, GROUP), lambda g: (0, g)),
        ],
        out_specs=[
            whole(long, width),
            whole(2, rows, 2 * STATE),
            whole(2, rows, LANES),
            whole(2, rows, LANES),
            whole(2, LANES, rows),
            pl.BlockSpec((2, 1, rows, GROUP), lambda g: (0, g, 0, 0)),
            pl.BlockSpec((2, 1, STATE, GROUP), lambda g: (0, g, 0, 0)),
            pl.BlockSpec((2, 1, 8, GROUP), lambda g: (0, g, 0, 0)),
        ],
        scratch_shapes=[
            pltpu.VMEM((2, 8, LANES), f32),
            pltpu.VMEM((2, rows, LANES), f32),
            pltpu.VMEM((2, 2 * rows, LANES), f32),
        ],
        compiler_params=pltpu.CompilerParams(vmem_limit_bytes=48 * 2**20),
        cost_estimate=pl.CostEstimate(flops=4_200_000_000, bytes_accessed=14_000_000, transcendentals=2_000_000),
        name="project_x",
    )(
        hidden,
        prev,
        follow,
        norm_gain[None],
        bc_weight,
        dt_weight,
        bc_kernel,
        dt_bias[None],
        log_rate[None],
        x_weight,
        x_kernel,
    )
    block = width // n_head
    vmem = pl.BlockSpec(memory_space=pltpu.VMEM)
    hbm = pl.BlockSpec(memory_space=pl.ANY)
    return pl.pallas_call(
        functools.partial(second_kernel, n_ctx, ("ctx", "head")),
        out_shape=jax.ShapeDtypeStruct((rows, block), hidden.dtype),
        in_specs=[vmem] * 10 + [hbm] * 2,
        out_specs=vmem,
        scratch_shapes=[
            pltpu.VMEM((groups, width, GROUP), bf16),
            pltpu.VMEM((inner, width), bf16),
            pltpu.VMEM((groups, 2 * rows, GROUP), bf16),
            pltpu.VMEM((groups, 2, rows, GROUP), f32),
            pltpu.VMEM((2, rows, inner), bf16),
            pltpu.VMEM((2, rows, rows), f32),
            pltpu.VMEM((2, groups, STATE, GROUP), bf16),
            pltpu.VMEM((2, groups, STATE, GROUP), bf16),
            pltpu.VMEM((2, rows, block), bf16),
            pltpu.VMEM((2, rows, block), bf16),
            pltpu.VMEM((rows, block), bf16),
            pltpu.VMEM((rows, block), bf16),
            pltpu.SemaphoreType.DMA((groups,)),
            pltpu.SemaphoreType.DMA,
            pltpu.SemaphoreType.DMA((2, groups)),
            pltpu.SemaphoreType.DMA((2, groups)),
            pltpu.SemaphoreType.DMA((3,)),
            pltpu.SemaphoreType.DMA((3,)),
        ],
        compiler_params=pltpu.CompilerParams(
            collective_id=0, has_side_effects=True, vmem_limit_bytes=56 * 2**20
        ),
        cost_estimate=pl.CostEstimate(flops=8_000_000_000, bytes_accessed=20_000_000, transcendentals=3_000_000),
        name="mix_and_project",
    )(*made, out_gain[None], hidden, z_weight, out_weight)


def solution(mesh):
    return jax.shard_map(
        functools.partial(per_device, mesh),
        mesh=mesh,
        in_specs=(
            P("ctx", None),
            P(),
            P(None, "head"),
            P(None, "head"),
            P(),
            P(None, "head"),
            P(None, "head"),
            P(),
            P("head"),
            P("head"),
            P("head"),
            P("head", None),
        ),
        out_specs=P("ctx", "head"),
        check_vma=False,
    )
```

```python
import functools

import jax
import jax.numpy as jnp
from jax import lax
from jax.experimental import pallas as pl
from jax.experimental.pallas import tpu as pltpu
from jax.sharding import PartitionSpec as P

HEAD_DIM = 64
STATE = 128
GROUP = 256
LANES = 128
HALO = 16
epsilon = 1e-05
highest = lax.Precision.HIGHEST
MESH = pl.DeviceIdType.MESH
f32 = jnp.float32
bf16 = jnp.bfloat16


def iota(shape, dim):
    return lax.broadcasted_iota(jnp.int32, shape, dim)


def dot(a, b, precision=None):
    return jnp.dot(a, b, preferred_element_type=f32, precision=precision)


def silu(v):
    return v / (1.0 + jnp.exp(-v))


def anti(size):
    return (iota((size, size), 0) + iota((size, size), 1) == size - 1).astype(bf16)


def spread(group):
    head = group * (GROUP // HEAD_DIM) + iota((LANES, GROUP), 1) // HEAD_DIM
    return (iota((LANES, GROUP), 0) == head).astype(f32)


def conv_fwd(ext, taps, rows):
    out = taps[0:1] * ext[HALO - 3 : HALO - 3 + rows]
    for k in range(1, 4):
        out = out + taps[k : k + 1] * ext[HALO - 3 + k : HALO - 3 + k + rows]
    return silu(out).astype(bf16)


def conv_bwd(ext, taps, rows):
    out = taps[0:1] * ext[3 : 3 + rows]
    for k in range(1, 4):
        out = out + taps[k : k + 1] * ext[3 - k : 3 - k + rows]
    return silu(out).astype(bf16)


def kernel(
    n_ctx, axes,
    gain_ref, dtw_ref, xk_ref, bck_ref, dtb_ref, rate_ref, out_gain_ref, h_hbm, xw_hbm, zw_hbm, bcw_hbm, ow_hbm,
    out_ref,
    h_buf, prev, follow, bcw, xw, zw, ow, n_buf, pad, bc, delta, cum, cumt, wend, dec, pair_dec,
    x_buf, z_buf, y_buf, gated, gram, state, pair_state, chain_in, carry, send_buf,
    one_send, one_recv, two_send, two_recv,
    in_sem, xw_sem, zw_sem, halo_send, halo_recv, d_send, d_recv, p_send, p_recv, c_send, c_recv, f_send, f_recv,
    r_send, r_recv,
):
    ctx_axis, head_axis = axes
    me = lax.axis_index(ctx_axis)
    place = lax.axis_index(head_axis)
    rows, width = h_buf.shape
    groups = x_buf.shape[1]
    block = out_ref.shape[1]
    ext = rows + HALO
    core = lax.rem(place, 2)
    side = place // 2
    sibling = side * 2 + (1 - core)
    across = (1 - side) * 2 + core
    other = lax.rem(me, 2)
    mine = 1 - other
    partner = me + 1 - 2 * other
    target = me + 2 - 4 * mine
    source = me - 2 + 4 * mine
    has_source = jnp.logical_and(source >= 0, source < n_ctx)
    has_target = jnp.logical_and(target >= 0, target < n_ctx)
    their_source = partner - 2 + 4 * other
    other_source = jnp.logical_and(their_source >= 0, their_source < n_ctx)

    def weight_copy(hbm, buf, sem, g):
        lanes = pl.ds(pl.multiple_of(g * GROUP, GROUP), GROUP)
        return pltpu.make_async_copy(hbm.at[:, lanes], buf.at[g], sem.at[g])

    h_copy = pltpu.make_async_copy(h_hbm, h_buf, in_sem.at[0])
    bc_copy = pltpu.make_async_copy(bcw_hbm, bcw, in_sem.at[1])
    o_copy = pltpu.make_async_copy(ow_hbm, ow, in_sem.at[2])
    h_copy.start()
    bc_copy.start()
    for g in range(groups):
        weight_copy(xw_hbm, xw, xw_sem, g).start()
    for g in range(groups):
        weight_copy(zw_hbm, zw, zw_sem, g).start()
    o_copy.start()

    barrier = pltpu.get_barrier_semaphore()
    for peer in (sibling, across):
        pl.semaphore_signal(barrier, inc=1, device_id={head_axis: peer}, device_id_type=MESH)
    peers = 2
    for hop in (-2, -1, 1, 2):
        present = jnp.logical_and(me + hop >= 0, me + hop < n_ctx)
        peers = peers + jnp.where(present, 1, 0)

        @pl.when(present)
        def _():
            pl.semaphore_signal(barrier, inc=1, device_id={ctx_axis: me + hop}, device_id_type=MESH)

    pl.semaphore_wait(barrier, peers)

    def remote(src, dst, send, recv, to):
        return pltpu.make_async_remote_copy(
            src_ref=src, dst_ref=dst, send_sem=send, recv_sem=recv,
            device_id={ctx_axis: to}, device_id_type=MESH,
        )

    def halo_copy(way, to):
        first = rows - HALO if way == 0 else 0
        return remote(
            h_hbm.at[pl.ds(first, HALO), :], prev if way == 0 else follow,
            halo_send.at[way], halo_recv.at[way], to,
        )

    def decay_copy():
        return remote(dec.at[other], pair_dec, d_send, d_recv, partner)

    def pair_copy(g):
        return remote(state.at[other, g], pair_state.at[g], p_send.at[g], p_recv.at[g], partner)

    def chain_copy(g):
        return remote(send_buf.at[g], chain_in.at[g], c_send.at[g], c_recv.at[g], target)

    def hand_copy(d, g):
        return remote(chain_in.at[g], carry.at[d, g], f_send.at[g], f_recv.at[g], partner)

    @pl.when(me < n_ctx - 1)
    def _():
        halo_copy(0, me + 1).start()

    @pl.when(me > 0)
    def _():
        halo_copy(1, me - 1).start()

    gain = gain_ref[...].reshape(1, width)
    blocks = width // GROUP
    turn = anti(GROUP)

    def turned(ref):
        return jnp.concatenate(
            [dot(ref[:, (blocks - 1 - j) * GROUP : (blocks - j) * GROUP], turn) for j in range(blocks)], axis=1
        )

    def scale(u):
        return lax.rsqrt(jnp.mean(u * u, axis=1, keepdims=True) + epsilon)

    h_copy.wait()
    here = h_buf[...].astype(f32)
    factor = scale(here)
    n_buf[HALO:ext, :] = (here * factor * gain).astype(bf16)
    n_buf[ext : ext + rows, :] = (turned(h_buf) * factor * gain).astype(bf16)

    @pl.when(me > 0)
    def _():
        halo_copy(0, me - 1).wait_recv()

    @pl.when(me == 0)
    def _():
        prev[...] = jnp.zeros_like(prev)

    @pl.when(me < n_ctx - 1)
    def _():
        halo_copy(1, me + 1).wait_recv()

    @pl.when(me == n_ctx - 1)
    def _():
        follow[...] = jnp.zeros_like(follow)

    prior = prev[...].astype(f32)
    n_buf[0:HALO, :] = (prior * scale(prior) * gain).astype(bf16)
    later = turned(follow)
    n_buf[ext + rows :, :] = (later * scale(later) * gain).astype(bf16)

    bc_copy.wait()
    bc_in = dot(n_buf[...], bcw[...]).astype(bf16).astype(f32)
    bc[0] = conv_fwd(bc_in[:ext], bck_ref[...], rows)
    bc[1] = conv_bwd(bc_in[ext:], bck_ref[...], rows)
    raw = lax.dot_general(
        n_buf[HALO : ext + rows, :], dtw_ref[...], (((1,), (1,)), ((), ())), preferred_element_type=f32
    ) + dtb_ref[...]
    step = jnp.maximum(raw, 0.0) + jnp.log1p(jnp.exp(-jnp.abs(raw)))
    heads = raw.shape[1]
    pad[...] = jnp.zeros_like(pad)
    pad[0, :, 0:heads] = step
    pad[1, :, 0:heads] = -step * jnp.exp(rate_ref[...])
    ahead_rows = iota((rows, rows), 0) - iota((rows, rows), 1)
    for d in range(2):
        part = slice(d * rows, (d + 1) * rows)
        mask = ahead_rows >= 0 if d == 0 else ahead_rows <= 0
        total = dot(mask.astype(f32), pad[1, part, :], highest)
        end = total[rows - 1 : rows] if d == 0 else total[0:1]
        delta[d] = pad[0, part, :]
        cum[d] = total
        cumt[d] = total.T
        wend[d] = jnp.exp(end - total) * pad[0, part, :]
        last = jnp.broadcast_to(jnp.exp(end), (8, LANES))
        for g in range(groups):
            dec[d, g] = dot(last, spread(g), highest)
    decay_copy().start()

    def x_unit(g, _):
        weight_copy(xw_hbm, xw, xw_sem, g).wait()
        x_in = dot(n_buf[...], xw[g]).astype(bf16).astype(f32)
        taps = xk_ref[:, pl.ds(pl.multiple_of(g * GROUP, GROUP), GROUP)]
        hot = spread(g)
        for d in range(2):
            x_conv = conv_fwd(x_in[:ext], taps, rows) if d == 0 else conv_bwd(x_in[ext:], taps, rows)
            x_buf[d, g] = x_conv
            weighted = (x_conv.astype(f32) * dot(wend[d], hot, highest)).astype(bf16)
            state[d, g] = lax.dot_general(
                bc[d, :, :STATE], weighted, (((0,), (0,)), ((), ())), preferred_element_type=f32
            ).astype(bf16)
        pair_copy(g).start()
        return 0

    lax.fori_loop(0, groups, x_unit, 0)

    for d in range(2):
        full = lax.dot_general(
            bc[d, :, STATE:], bc[d, :, :STATE], (((1,), (1,)), ((), ())), preferred_element_type=f32
        )
        gram[d] = jnp.where(ahead_rows >= 0 if d == 0 else ahead_rows <= 0, full, 0.0)

    def unit(g, _):
        weight_copy(zw_hbm, zw, zw_sem, g).wait()
        z_buf[g] = dot(n_buf[HALO : HALO + 2 * rows, :], zw[g]).astype(bf16)
        hot = spread(g)
        lane_head = iota((rows, GROUP), 1) // HEAD_DIM
        for d in range(2):
            scaled = x_buf[d, g].astype(f32) * dot(delta[d], hot, highest)
            cols = dot(cum[d], hot, highest)
            parts, values = [], []
            for j in range(GROUP // HEAD_DIM):
                column = cols[:, j * HEAD_DIM : j * HEAD_DIM + 1]
                row = cumt[d, pl.ds(g * (GROUP // HEAD_DIM) + j, 1), :]
                parts.append((jnp.exp(jnp.minimum(column - row, 0.0)) * gram[d]).astype(bf16))
                values.append(jnp.where(lane_head == j, scaled, 0.0).astype(bf16))
            y_buf[g, d] = dot(jnp.concatenate(parts, axis=1), jnp.concatenate(values, axis=0))
        return 0

    def chain(g, _):
        pair_copy(g).wait_recv()

        @pl.when(has_source)
        def _():
            chain_copy(g).wait_recv()

        @pl.when(jnp.logical_not(has_source))
        def _():
            chain_in[g] = jnp.zeros_like(chain_in[g])

        joined = chain_in[g].astype(f32) * pair_dec[g, 0:1, :] + pair_state[g].astype(f32)
        carry[mine, g] = joined.astype(bf16)

        @pl.when(has_target)
        def _():
            send_buf[g] = (joined * dec[mine, g, 0:1, :] + state[mine, g].astype(f32)).astype(bf16)
            chain_copy(g).start()

        @pl.when(has_source)
        def _():
            hand_copy(mine, g).start()

        return 0

    late = jnp.where(mine == 0, me // 2, n_ctx // 2 - 1 - me // 2)
    before = jnp.minimum(groups, late + jnp.where(late > 1, 1, 0))
    lax.fori_loop(0, before, unit, 0)
    decay_copy().wait_recv()
    lax.fori_loop(0, groups, chain, 0)
    lax.fori_loop(before, groups, unit, 0)

    out_gain = out_gain_ref[...].reshape(1, groups * GROUP)
    same = iota((GROUP, GROUP), 0) // HEAD_DIM == iota((GROUP, GROUP), 1) // HEAD_DIM
    average = jnp.where(same, 1.0 / HEAD_DIM, 0.0).astype(bf16)
    growth = [jnp.exp(cum[d]) for d in range(2)]
    for g in range(groups):
        hot = spread(g)

        @pl.when(other_source)
        def _():
            hand_copy(other, g).wait_recv()

        @pl.when(jnp.logical_not(other_source))
        def _():
            carry[other, g] = jnp.zeros_like(carry[other, g])

        for d in range(2):
            carried = dot(bc[d, :, STATE:], carry[d, g]) * dot(growth[d], hot, highest)
            value = (y_buf[g, d] + carried) * silu(z_buf[g, d * rows : (d + 1) * rows].astype(f32))
            square = value * value
            high = square.astype(bf16)
            low = (square - high.astype(f32)).astype(bf16)
            mean_sq = dot(high, average) + dot(low, average)
            lanes = slice(g * GROUP, (g + 1) * GROUP)
            gated[d, :, lanes] = (
                value * lax.rsqrt(mean_sq + epsilon) * out_gain[:, lanes]
            ).astype(bf16)

    o_copy.wait()
    flip = anti(LANES)
    blocks = ow_hbm.shape[1] // block

    def project(which):
        mine = pl.multiple_of(which * block, LANES)
        other = pl.multiple_of((blocks - 1 - which) * block, LANES)
        ahead = dot(gated[0], ow[:, pl.ds(mine, block)])
        back = dot(gated[1], ow[:, pl.ds(other, block)]).astype(bf16)
        count = block // LANES
        turned = [
            dot(back[:, (count - 1 - j) * LANES : (count - j) * LANES], flip) for j in range(count)
        ]
        return ahead + jnp.concatenate(turned, axis=1)

    def near(slot):
        return pltpu.make_async_remote_copy(
            src_ref=one_send.at[slot],
            dst_ref=one_recv.at[slot],
            send_sem=r_send.at[slot],
            recv_sem=r_recv.at[slot],
            device_id={head_axis: sibling},
            device_id_type=MESH,
        )

    far = pltpu.make_async_remote_copy(
        src_ref=two_send,
        dst_ref=two_recv,
        send_sem=r_send.at[2],
        recv_sem=r_recv.at[2],
        device_id={head_axis: across},
        device_id_type=MESH,
    )
    one_send[0] = project((1 - side) * 2 + (1 - core)).astype(bf16)
    near(0).start()
    partial = project(across)
    near(0).wait_recv()
    two_send[...] = (partial + one_recv[0].astype(f32)).astype(bf16)
    far.start()
    one_send[1] = project(sibling).astype(bf16)
    near(1).start()
    partial = project(place)
    residual = h_buf[:, pl.ds(pl.multiple_of(place * block, LANES), block)].astype(f32)
    near(1).wait_recv()
    partial = partial + one_recv[1].astype(f32)
    far.wait_recv()
    out_ref[...] = (residual + (partial + two_recv[...].astype(f32))).astype(out_ref.dtype)
    near(0).wait_send()
    near(1).wait_send()
    far.wait_send()


    @pl.when(me < n_ctx - 1)
    def _():
        halo_copy(0, me + 1).wait_send()

    @pl.when(me > 0)
    def _():
        halo_copy(1, me - 1).wait_send()

    decay_copy().wait_send()

    def drain(g, _):
        pair_copy(g).wait_send()

        @pl.when(has_target)
        def _():
            chain_copy(g).wait_send()

        @pl.when(has_source)
        def _():
            hand_copy(mine, g).wait_send()

        return 0

    lax.fori_loop(0, groups, drain, 0)


def per_device(
    mesh,
    hidden,
    norm_gain,
    x_weight,
    z_weight,
    bc_weight,
    dt_weight,
    x_kernel,
    bc_kernel,
    dt_bias,
    log_rate,
    out_gain,
    out_weight,
):
    rows, width = hidden.shape
    inner = x_weight.shape[1]
    groups = inner // GROUP
    block = width // mesh.shape["head"]
    ext = rows + HALO
    vmem = pl.BlockSpec(memory_space=pltpu.VMEM)
    hbm = pl.BlockSpec(memory_space=pl.ANY)
    dma = pltpu.SemaphoreType.DMA
    return pl.pallas_call(
        functools.partial(kernel, mesh.shape["ctx"], ("ctx", "head")),
        out_shape=jax.ShapeDtypeStruct((rows, block), hidden.dtype),
        in_specs=[vmem] * 7 + [hbm] * 5,
        out_specs=vmem,
        scratch_shapes=[
            pltpu.VMEM((rows, width), bf16),
            pltpu.VMEM((HALO, width), bf16),
            pltpu.VMEM((HALO, width), bf16),
            pltpu.VMEM((width, 2 * STATE), bf16),
            pltpu.VMEM((groups, width, GROUP), bf16),
            pltpu.VMEM((groups, width, GROUP), bf16),
            pltpu.VMEM((inner, width), bf16),
            pltpu.VMEM((2 * ext, width), bf16),
            pltpu.VMEM((2, 2 * rows, LANES), f32),
            pltpu.VMEM((2, rows, 2 * STATE), bf16),
            pltpu.VMEM((2, rows, LANES), f32),
            pltpu.VMEM((2, rows, LANES), f32),
            pltpu.VMEM((2, LANES, rows), f32),
            pltpu.VMEM((2, rows, LANES), f32),
            pltpu.VMEM((2, groups, 8, GROUP), f32),
            pltpu.VMEM((groups, 8, GROUP), f32),
            pltpu.VMEM((2, groups, rows, GROUP), bf16),
            pltpu.VMEM((groups, 2 * rows, GROUP), bf16),
            pltpu.VMEM((groups, 2, rows, GROUP), f32),
            pltpu.VMEM((2, rows, inner), bf16),
            pltpu.VMEM((2, rows, rows), f32),
            pltpu.VMEM((2, groups, STATE, GROUP), bf16),
            pltpu.VMEM((groups, STATE, GROUP), bf16),
            pltpu.VMEM((groups, STATE, GROUP), bf16),
            pltpu.VMEM((2, groups, STATE, GROUP), bf16),
            pltpu.VMEM((groups, STATE, GROUP), bf16),
            pltpu.VMEM((2, rows, block), bf16),
            pltpu.VMEM((2, rows, block), bf16),
            pltpu.VMEM((rows, block), bf16),
            pltpu.VMEM((rows, block), bf16),
            dma((3,)),
            dma((groups,)),
            dma((groups,)),
            dma((2,)),
            dma((2,)),
            dma,
            dma,
            dma((groups,)),
            dma((groups,)),
            dma((groups,)),
            dma((groups,)),
            dma((groups,)),
            dma((groups,)),
            dma((3,)),
            dma((3,)),
        ],
        compiler_params=pltpu.CompilerParams(
            collective_id=0, has_side_effects=True, vmem_limit_bytes=60 * 2**20
        ),
        cost_estimate=pl.CostEstimate(flops=12_000_000_000, bytes_accessed=24_000_000, transcendentals=5_000_000),
        name="mixer",
    )(
        norm_gain,
        dt_weight.T,
        x_kernel,
        bc_kernel,
        dt_bias[None],
        log_rate[None],
        out_gain,
        hidden,
        x_weight,
        z_weight,
        bc_weight,
        out_weight,
    )


def solution(mesh):
    return jax.shard_map(
        functools.partial(per_device, mesh),
        mesh=mesh,
        in_specs=(
            P("ctx", None),
            P(),
            P(None, "head"),
            P(None, "head"),
            P(),
            P(None, "head"),
            P(None, "head"),
            P(),
            P("head"),
            P("head"),
            P("head"),
            P("head", None),
        ),
        out_specs=P("ctx", "head"),
        check_vma=False,
    )
```

```python
import functools

import jax
import jax.numpy as jnp
from jax import lax
from jax.experimental import pallas as pl
from jax.experimental.pallas import tpu as pltpu
from jax.sharding import PartitionSpec as P

HEAD_DIM = 64
STATE = 128
GROUP = 256
LANES = 128
HALO = 16
epsilon = 1e-05
highest = lax.Precision.HIGHEST
MESH = pl.DeviceIdType.MESH
f32 = jnp.float32
bf16 = jnp.bfloat16


def iota(shape, dim):
    return lax.broadcasted_iota(jnp.int32, shape, dim)


def dot(a, b, precision=None):
    return jnp.dot(a, b, preferred_element_type=f32, precision=precision)


def silu(v):
    half = 0.5 * v
    return half + half * jnp.tanh(half)


def pieces(v, count):
    out = []
    for _ in range(count):
        part = v.astype(bf16)
        out.append(part)
        v = v - part.astype(f32)
    return jnp.concatenate(out, axis=1)


def anti(size):
    return (iota((size, size), 0) + iota((size, size), 1) == size - 1).astype(bf16)


def spread(group, count=2, each=HEAD_DIM):
    per = GROUP // HEAD_DIM
    shape = (count * LANES, per * each)
    head = group * per + iota(shape, 1) // each
    return (lax.rem(iota(shape, 0), LANES) == head).astype(bf16)


def conv_fwd(ext, taps, rows):
    out = taps[0:1] * ext[HALO - 3 : HALO - 3 + rows]
    for k in range(1, 4):
        out = out + taps[k : k + 1] * ext[HALO - 3 + k : HALO - 3 + k + rows]
    return silu(out).astype(bf16)


def conv_bwd(ext, taps, rows):
    out = taps[0:1] * ext[3 : 3 + rows]
    for k in range(1, 4):
        out = out + taps[k : k + 1] * ext[3 - k : 3 - k + rows]
    return silu(out).astype(bf16)


def kernel(
    n_ctx, axes,
    gain_ref, dtw_ref, xk_ref, bck_ref, dtb_ref, rate_ref, out_gain_ref, h_hbm, xw_hbm, zw_hbm, bcw_hbm, ow_hbm,
    out_ref,
    h_buf, prev, follow, bcw, xw, zw, ow, n_buf, pad, bc, delta, cum, cumt, wend, growth, mid, dec, pair_dec, x_in, out_gain,
    x_buf, z_buf, y_buf, gated, gram, state, pair_state, chain_in, carry, send_buf,
    one_send, one_recv, two_send, two_recv,
    in_sem, xw_sem, zw_sem, halo_send, halo_recv, d_send, d_recv, p_send, p_recv, c_send, c_recv, f_send, f_recv,
    r_send, r_recv,
):
    ctx_axis, head_axis = axes
    me = lax.axis_index(ctx_axis)
    place = lax.axis_index(head_axis)
    rows, width = h_buf.shape
    groups = x_buf.shape[1]
    block = out_ref.shape[1]
    ext = rows + HALO
    half = rows // 2
    core = lax.rem(place, 2)
    side = place // 2
    sibling = side * 2 + (1 - core)
    across = (1 - side) * 2 + core
    other = lax.rem(me, 2)
    mine = 1 - other
    partner = me + 1 - 2 * other
    target = me + 2 - 4 * mine
    source = me - 2 + 4 * mine
    has_source = jnp.logical_and(source >= 0, source < n_ctx)
    has_target = jnp.logical_and(target >= 0, target < n_ctx)
    their_source = partner - 2 + 4 * other
    other_source = jnp.logical_and(their_source >= 0, their_source < n_ctx)

    def weight_copy(hbm, buf, sem, g):
        lanes = pl.ds(pl.multiple_of(g * GROUP, GROUP), GROUP)
        return pltpu.make_async_copy(hbm.at[:, lanes], buf.at[g], sem.at[g])

    h_copy = pltpu.make_async_copy(h_hbm, h_buf, in_sem.at[0])
    bc_copy = pltpu.make_async_copy(bcw_hbm, bcw, in_sem.at[1])
    o_copy = pltpu.make_async_copy(ow_hbm, ow, in_sem.at[2])
    h_copy.start()
    bc_copy.start()
    for g in range(groups):
        weight_copy(xw_hbm, xw, xw_sem, g).start()
    for g in range(groups):
        weight_copy(zw_hbm, zw, zw_sem, g).start()
    o_copy.start()

    barrier = pltpu.get_barrier_semaphore()
    for peer in (sibling, across):
        pl.semaphore_signal(barrier, inc=1, device_id={head_axis: peer}, device_id_type=MESH)
    peers = 2
    for hop in (-2, -1, 1, 2):
        present = jnp.logical_and(me + hop >= 0, me + hop < n_ctx)
        peers = peers + jnp.where(present, 1, 0)

        @pl.when(present)
        def _():
            pl.semaphore_signal(barrier, inc=1, device_id={ctx_axis: me + hop}, device_id_type=MESH)

    pl.semaphore_wait(barrier, peers)

    def remote(src, dst, send, recv, to):
        return pltpu.make_async_remote_copy(
            src_ref=src, dst_ref=dst, send_sem=send, recv_sem=recv,
            device_id={ctx_axis: to}, device_id_type=MESH,
        )

    def halo_copy(way, to):
        first = rows - HALO if way == 0 else 0
        return remote(
            h_hbm.at[pl.ds(first, HALO), :], prev if way == 0 else follow,
            halo_send.at[way], halo_recv.at[way], to,
        )

    def decay_copy():
        return remote(dec.at[other], pair_dec, d_send, d_recv, partner)

    def pair_copy(g):
        return remote(state.at[other, g], pair_state.at[g], p_send.at[g], p_recv.at[g], partner)

    def chain_copy(g):
        return remote(send_buf.at[g], chain_in.at[g], c_send.at[g], c_recv.at[g], target)

    def hand_copy(d, g):
        return remote(chain_in.at[g], carry.at[d, g], f_send.at[g], f_recv.at[g], partner)

    @pl.when(me < n_ctx - 1)
    def _():
        halo_copy(0, me + 1).start()

    @pl.when(me > 0)
    def _():
        halo_copy(1, me - 1).start()

    gain = gain_ref[...].reshape(1, width)
    blocks = width // GROUP
    turn = anti(GROUP)

    def turned(ref):
        return jnp.concatenate(
            [dot(ref[:, (blocks - 1 - j) * GROUP : (blocks - j) * GROUP], turn) for j in range(blocks)], axis=1
        )

    def scale(u):
        return lax.rsqrt(jnp.mean(u * u, axis=1, keepdims=True) + epsilon)

    h_copy.wait()
    here = h_buf[...].astype(f32)
    factor = scale(here)
    n_buf[HALO:ext, :] = (here * factor * gain).astype(bf16)
    n_buf[ext : ext + rows, :] = (turned(h_buf) * factor * gain).astype(bf16)

    @pl.when(me > 0)
    def _():
        halo_copy(0, me - 1).wait_recv()

    @pl.when(me == 0)
    def _():
        prev[...] = jnp.zeros_like(prev)

    @pl.when(me < n_ctx - 1)
    def _():
        halo_copy(1, me + 1).wait_recv()

    @pl.when(me == n_ctx - 1)
    def _():
        follow[...] = jnp.zeros_like(follow)

    prior = prev[...].astype(f32)
    n_buf[0:HALO, :] = (prior * scale(prior) * gain).astype(bf16)
    later = turned(follow)
    n_buf[ext + rows :, :] = (later * scale(later) * gain).astype(bf16)

    bc_copy.wait()
    bc_in = dot(n_buf[...], bcw[...]).astype(bf16).astype(f32)
    bc[0] = conv_fwd(bc_in[:ext], bck_ref[...], rows)
    bc[1] = conv_bwd(bc_in[ext:], bck_ref[...], rows)
    raw = lax.dot_general(
        n_buf[HALO : ext + rows, :], dtw_ref[...], (((1,), (1,)), ((), ())), preferred_element_type=f32
    ) + dtb_ref[...]
    step = jnp.maximum(raw, 0.0) + jnp.log1p(jnp.exp(-jnp.abs(raw)))
    heads = raw.shape[1]
    pad[...] = jnp.zeros_like(pad)
    pad[0, :, 0:heads] = step
    pad[1, :, 0:heads] = -step * jnp.exp(rate_ref[...])
    ahead_rows = iota((rows, rows), 0) - iota((rows, rows), 1)
    for d in range(2):
        part = slice(d * rows, (d + 1) * rows)
        mask = ahead_rows >= 0 if d == 0 else ahead_rows <= 0
        total = dot(mask.astype(f32), pad[1, part, :], highest)
        end = total[rows - 1 : rows] if d == 0 else total[0:1]
        cumt[d] = total.T
        step_d = pad[0, part, :]
        delta[d] = pieces(step_d, 2)
        cum[d] = pieces(total, 3)
        wend[d] = pieces(jnp.exp(end - total) * step_d, 2)
        growth[d] = pieces(jnp.exp(total), 2)
        edge = total[half - 1 : half] if d == 0 else total[half : half + 1]
        low_part, high_part = total[:half], total[half:]
        if d == 0:
            mids = [jnp.exp(edge - low_part) * step_d[:half], jnp.exp(high_part - edge)]
        else:
            mids = [jnp.exp(low_part - edge), jnp.exp(edge - high_part) * step_d[half:]]
        mid[d] = pieces(jnp.concatenate(mids, axis=0), 2)
        last = pieces(jnp.broadcast_to(jnp.exp(end), (8, LANES)), 3)
        for g in range(groups):
            dec[d, g] = dot(last, spread(g, 3))
    decay_copy().start()

    def x_project(g):
        weight_copy(xw_hbm, xw, xw_sem, g).wait()
        x_in[g % 2] = dot(n_buf[...], xw[g]).astype(bf16)

    x_project(0)
    for g in range(groups):
        if g + 1 < groups:
            x_project(g + 1)
        now = x_in[g % 2].astype(f32)
        taps = xk_ref[:, g * GROUP : (g + 1) * GROUP]
        hot = spread(g)
        for d in range(2):
            x_conv = conv_fwd(now[:ext], taps, rows) if d == 0 else conv_bwd(now[ext:], taps, rows)
            x_buf[d, g] = x_conv
            weighted = (x_conv.astype(f32) * dot(wend[d], hot)).astype(bf16)
            state[d, g] = lax.dot_general(
                bc[d, :, :STATE], weighted, (((0,), (0,)), ((), ())), preferred_element_type=f32
            ).astype(bf16)
        pair_copy(g).start()

    for d in range(2):
        full = lax.dot_general(
            bc[d, :, STATE:], bc[d, :, :STATE], (((1,), (1,)), ((), ())), preferred_element_type=f32
        )
        gram[d] = jnp.where(ahead_rows >= 0 if d == 0 else ahead_rows <= 0, full, 0.0)

    def unit(g, _):
        weight_copy(zw_hbm, zw, zw_sem, g).wait()
        z_in = dot(n_buf[HALO : HALO + 2 * rows, :], zw[g]).astype(bf16)
        z_buf[g, 0] = z_in[:rows]
        z_buf[g, 1] = z_in[rows:]
        hot = spread(g)
        wide = spread(g, 3, half)
        per = GROUP // HEAD_DIM
        lane_head = iota((half, GROUP), 1) // HEAD_DIM
        for d in range(2):
            x_here = x_buf[d, g].astype(f32)
            scaled = x_here * dot(delta[d], hot)
            cols = dot(cum[d], wide)
            middle = dot(mid[d], hot)
            for b in range(2):
                here = slice(b * half, (b + 1) * half)
                there = slice((1 - b) * half, (2 - b) * half)
                parts, values = [], []
                for j in range(per):
                    column = cols[here, j * half : (j + 1) * half]
                    row = cumt[d, pl.ds(g * per + j, 1), :][:, here]
                    parts.append((jnp.exp(jnp.minimum(column - row, 0.0)) * gram[d, here, here]).astype(bf16))
                    values.append(jnp.where(lane_head == j, scaled[here], 0.0).astype(bf16))
                y = dot(jnp.concatenate(parts, axis=1), jnp.concatenate(values, axis=0))
                if b != d:
                    sent = (x_here[there] * middle[there]).astype(bf16)
                    y = y + middle[here] * dot(gram[d, here, there].astype(bf16), sent)
                y_buf[g, d, here] = y
        return 0

    def chain(g, _):
        pair_copy(g).wait_recv()

        @pl.when(has_source)
        def _():
            chain_copy(g).wait_recv()

        @pl.when(jnp.logical_not(has_source))
        def _():
            chain_in[g] = jnp.zeros_like(chain_in[g])

        joined = chain_in[g].astype(f32) * pair_dec[g, 0:1, :] + pair_state[g].astype(f32)
        carry[mine, g] = joined.astype(bf16)

        @pl.when(has_target)
        def _():
            send_buf[g] = (joined * dec[mine, g, 0:1, :] + state[mine, g].astype(f32)).astype(bf16)
            chain_copy(g).start()

        @pl.when(has_source)
        def _():
            hand_copy(mine, g).start()

        return 0

    late = jnp.where(mine == 0, me // 2, n_ctx // 2 - 1 - me // 2)
    before = jnp.minimum(groups, late + jnp.where(late > 1, 1, 0))
    lax.fori_loop(0, before, unit, 0)
    decay_copy().wait_recv()
    lax.fori_loop(0, groups, chain, 0)
    lax.fori_loop(before, groups, unit, 0)

    same = iota((GROUP, GROUP), 0) // HEAD_DIM == iota((GROUP, GROUP), 1) // HEAD_DIM
    average = jnp.where(same, 1.0 / HEAD_DIM, 0.0).astype(bf16)
    out_gain[...] = out_gain_ref[...].reshape(1, groups * GROUP)

    def finish(d, g):
        carried = dot(bc[d, :, STATE:], carry[d, g]) * dot(growth[d], spread(g))
        value = (y_buf[g, d] + carried) * silu(z_buf[g, d].astype(f32))
        square = value * value
        high = square.astype(bf16)
        low = (square - high.astype(f32)).astype(bf16)
        mean_sq = dot(high, average) + dot(low, average)
        lanes = pl.ds(pl.multiple_of(g * GROUP, GROUP), GROUP)
        gated[d, :, lanes] = (value * lax.rsqrt(mean_sq + epsilon) * out_gain[:, lanes]).astype(bf16)

    def finish_mine(g, _):
        finish(mine, g)
        return 0

    def finish_other(g, _):
        @pl.when(other_source)
        def _():
            hand_copy(other, g).wait_recv()

        @pl.when(jnp.logical_not(other_source))
        def _():
            carry[other, g] = jnp.zeros_like(carry[other, g])

        finish(other, g)
        return 0

    lax.fori_loop(0, groups, finish_mine, 0)
    lax.fori_loop(0, groups, finish_other, 0)

    o_copy.wait()
    flip = anti(LANES)
    blocks = ow_hbm.shape[1] // block

    def project(which):
        mine = pl.multiple_of(which * block, LANES)
        other = pl.multiple_of((blocks - 1 - which) * block, LANES)
        ahead = dot(gated[0], ow[:, pl.ds(mine, block)])
        back = dot(gated[1], ow[:, pl.ds(other, block)]).astype(bf16)
        count = block // LANES
        turned = [
            dot(back[:, (count - 1 - j) * LANES : (count - j) * LANES], flip) for j in range(count)
        ]
        return ahead + jnp.concatenate(turned, axis=1)

    def near(slot):
        return pltpu.make_async_remote_copy(
            src_ref=one_send.at[slot],
            dst_ref=one_recv.at[slot],
            send_sem=r_send.at[slot],
            recv_sem=r_recv.at[slot],
            device_id={head_axis: sibling},
            device_id_type=MESH,
        )

    far = pltpu.make_async_remote_copy(
        src_ref=two_send,
        dst_ref=two_recv,
        send_sem=r_send.at[2],
        recv_sem=r_recv.at[2],
        device_id={head_axis: across},
        device_id_type=MESH,
    )
    one_send[0] = project((1 - side) * 2 + (1 - core)).astype(bf16)
    near(0).start()
    partial = project(across)
    near(0).wait_recv()
    two_send[...] = (partial + one_recv[0].astype(f32)).astype(bf16)
    far.start()
    one_send[1] = project(sibling).astype(bf16)
    near(1).start()
    partial = project(place)
    residual = h_buf[:, pl.ds(pl.multiple_of(place * block, LANES), block)].astype(f32)
    near(1).wait_recv()
    partial = partial + one_recv[1].astype(f32)
    far.wait_recv()
    out_ref[...] = (residual + (partial + two_recv[...].astype(f32))).astype(out_ref.dtype)
    near(0).wait_send()
    near(1).wait_send()
    far.wait_send()


    @pl.when(me < n_ctx - 1)
    def _():
        halo_copy(0, me + 1).wait_send()

    @pl.when(me > 0)
    def _():
        halo_copy(1, me - 1).wait_send()

    decay_copy().wait_send()

    def drain(g, _):
        pair_copy(g).wait_send()

        @pl.when(has_target)
        def _():
            chain_copy(g).wait_send()

        @pl.when(has_source)
        def _():
            hand_copy(mine, g).wait_send()

        return 0

    lax.fori_loop(0, groups, drain, 0)


def per_device(
    mesh,
    hidden,
    norm_gain,
    x_weight,
    z_weight,
    bc_weight,
    dt_weight,
    x_kernel,
    bc_kernel,
    dt_bias,
    log_rate,
    out_gain,
    out_weight,
):
    rows, width = hidden.shape
    inner = x_weight.shape[1]
    groups = inner // GROUP
    block = width // mesh.shape["head"]
    ext = rows + HALO
    vmem = pl.BlockSpec(memory_space=pltpu.VMEM)
    hbm = pl.BlockSpec(memory_space=pl.ANY)
    dma = pltpu.SemaphoreType.DMA
    return pl.pallas_call(
        functools.partial(kernel, mesh.shape["ctx"], ("ctx", "head")),
        out_shape=jax.ShapeDtypeStruct((rows, block), hidden.dtype),
        in_specs=[vmem] * 7 + [hbm] * 5,
        out_specs=vmem,
        scratch_shapes=[
            pltpu.VMEM((rows, width), bf16),
            pltpu.VMEM((HALO, width), bf16),
            pltpu.VMEM((HALO, width), bf16),
            pltpu.VMEM((width, 2 * STATE), bf16),
            pltpu.VMEM((groups, width, GROUP), bf16),
            pltpu.VMEM((groups, width, GROUP), bf16),
            pltpu.VMEM((inner, width), bf16),
            pltpu.VMEM((2 * ext, width), bf16),
            pltpu.VMEM((2, 2 * rows, LANES), f32),
            pltpu.VMEM((2, rows, 2 * STATE), bf16),
            pltpu.VMEM((2, rows, 2 * LANES), bf16),
            pltpu.VMEM((2, rows, 3 * LANES), bf16),
            pltpu.VMEM((2, LANES, rows), f32),
            pltpu.VMEM((2, rows, 2 * LANES), bf16),
            pltpu.VMEM((2, rows, 2 * LANES), bf16),
            pltpu.VMEM((2, rows, 2 * LANES), bf16),
            pltpu.VMEM((2, groups, 8, GROUP), f32),
            pltpu.VMEM((groups, 8, GROUP), f32),
            pltpu.VMEM((2, 2 * ext, GROUP), bf16),
            pltpu.VMEM((1, inner), f32),
            pltpu.VMEM((2, groups, rows, GROUP), bf16),
            pltpu.VMEM((groups, 2, rows, GROUP), bf16),
            pltpu.VMEM((groups, 2, rows, GROUP), f32),
            pltpu.VMEM((2, rows, inner), bf16),
            pltpu.VMEM((2, rows, rows), f32),
            pltpu.VMEM((2, groups, STATE, GROUP), bf16),
            pltpu.VMEM((groups, STATE, GROUP), bf16),
            pltpu.VMEM((groups, STATE, GROUP), bf16),
            pltpu.VMEM((2, groups, STATE, GROUP), bf16),
            pltpu.VMEM((groups, STATE, GROUP), bf16),
            pltpu.VMEM((2, rows, block), bf16),
            pltpu.VMEM((2, rows, block), bf16),
            pltpu.VMEM((rows, block), bf16),
            pltpu.VMEM((rows, block), bf16),
            dma((3,)),
            dma((groups,)),
            dma((groups,)),
            dma((2,)),
            dma((2,)),
            dma,
            dma,
            dma((groups,)),
            dma((groups,)),
            dma((groups,)),
            dma((groups,)),
            dma((groups,)),
            dma((groups,)),
            dma((3,)),
            dma((3,)),
        ],
        compiler_params=pltpu.CompilerParams(
            collective_id=0, has_side_effects=True, vmem_limit_bytes=60 * 2**20
        ),
        cost_estimate=pl.CostEstimate(flops=12_000_000_000, bytes_accessed=24_000_000, transcendentals=5_000_000),
        name="mixer",
    )(
        norm_gain,
        dt_weight.T,
        x_kernel,
        bc_kernel,
        dt_bias[None],
        log_rate[None],
        out_gain,
        hidden,
        x_weight,
        z_weight,
        bc_weight,
        out_weight,
    )


def solution(mesh):
    return jax.shard_map(
        functools.partial(per_device, mesh),
        mesh=mesh,
        in_specs=(
            P("ctx", None),
            P(),
            P(None, "head"),
            P(None, "head"),
            P(),
            P(None, "head"),
            P(None, "head"),
            P(),
            P("head"),
            P("head"),
            P("head"),
            P("head", None),
        ),
        out_specs=P("ctx", "head"),
        check_vma=False,
    )
```

```python
import functools

import jax
import jax.numpy as jnp
from jax import lax
from jax.experimental import pallas as pl
from jax.experimental.pallas import tpu as pltpu
from jax.sharding import PartitionSpec as P

HEAD_DIM = 64
STATE = 128
GROUP = 256
LANES = 128
HALO = 16
epsilon = 1e-05
highest = lax.Precision.HIGHEST
MESH = pl.DeviceIdType.MESH
f32 = jnp.float32
bf16 = jnp.bfloat16


def iota(shape, dim):
    return lax.broadcasted_iota(jnp.int32, shape, dim)


def dot(a, b, precision=None):
    return jnp.dot(a, b, preferred_element_type=f32, precision=precision)


def silu(v):
    half = 0.5 * v
    return half + half * jnp.tanh(half)


def pieces(v, count):
    out = []
    for _ in range(count):
        part = v.astype(bf16)
        out.append(part)
        v = v - part.astype(f32)
    return jnp.concatenate(out, axis=1)


def anti(size):
    return (iota((size, size), 0) + iota((size, size), 1) == size - 1).astype(bf16)


def spread(group, count=2, each=HEAD_DIM):
    per = GROUP // HEAD_DIM
    shape = (count * LANES, per * each)
    head = group * per + iota(shape, 1) // each
    return (lax.rem(iota(shape, 0), LANES) == head).astype(bf16)


def conv_fwd(ext, taps, rows):
    out = taps[0:1] * ext[HALO - 3 : HALO - 3 + rows]
    for k in range(1, 4):
        out = out + taps[k : k + 1] * ext[HALO - 3 + k : HALO - 3 + k + rows]
    return silu(out).astype(bf16)


def conv_bwd(ext, taps, rows):
    out = taps[0:1] * ext[3 : 3 + rows]
    for k in range(1, 4):
        out = out + taps[k : k + 1] * ext[3 - k : 3 - k + rows]
    return silu(out).astype(bf16)


def kernel(
    n_ctx, axes,
    gain_ref, dtw_ref, xk_ref, bck_ref, dtb_ref, rate_ref, out_gain_ref, h_hbm, xw_hbm, zw_hbm, bcw_hbm, ow_hbm,
    out_ref,
    h_buf, prev, follow, bcw, xw, zw, ow, n_buf, pad, bc, delta, cum, cumt, wend, growth, mid, dec, pair_dec, x_in, out_gain,
    x_buf, z_buf, y_buf, gated, gram, state, pair_state, chain_in, carry, send_buf,
    one_send, one_recv, two_send, two_recv,
    in_sem, xw_sem, zw_sem, halo_send, halo_recv, d_send, d_recv, p_send, p_recv, c_send, c_recv, f_send, f_recv,
    r_send, r_recv,
):
    ctx_axis, head_axis = axes
    me = lax.axis_index(ctx_axis)
    place = lax.axis_index(head_axis)
    rows, width = h_buf.shape
    groups = x_buf.shape[1]
    block = out_ref.shape[1]
    ext = rows + HALO
    half = rows // 2
    core = lax.rem(place, 2)
    side = place // 2
    sibling = side * 2 + (1 - core)
    across = (1 - side) * 2 + core
    other = lax.rem(me, 2)
    mine = 1 - other
    partner = me + 1 - 2 * other
    target = me + 2 - 4 * mine
    source = me - 2 + 4 * mine
    has_source = jnp.logical_and(source >= 0, source < n_ctx)
    has_target = jnp.logical_and(target >= 0, target < n_ctx)
    their_source = partner - 2 + 4 * other
    other_source = jnp.logical_and(their_source >= 0, their_source < n_ctx)

    def weight_copy(hbm, buf, sem, g):
        lanes = pl.ds(pl.multiple_of(g * GROUP, GROUP), GROUP)
        return pltpu.make_async_copy(hbm.at[:, lanes], buf.at[g], sem.at[g])

    h_copy = pltpu.make_async_copy(h_hbm, h_buf, in_sem.at[0])
    bc_copy = pltpu.make_async_copy(bcw_hbm, bcw, in_sem.at[1])
    o_copy = pltpu.make_async_copy(ow_hbm, ow, in_sem.at[2])
    h_copy.start()
    bc_copy.start()
    for g in range(groups):
        weight_copy(xw_hbm, xw, xw_sem, g).start()
    for g in range(groups):
        weight_copy(zw_hbm, zw, zw_sem, g).start()
    o_copy.start()

    barrier = pltpu.get_barrier_semaphore()
    for peer in (sibling, across):
        pl.semaphore_signal(barrier, inc=1, device_id={head_axis: peer}, device_id_type=MESH)
    peers = 2
    for hop in (-2, -1, 1, 2):
        present = jnp.logical_and(me + hop >= 0, me + hop < n_ctx)
        peers = peers + jnp.where(present, 1, 0)

        @pl.when(present)
        def _():
            pl.semaphore_signal(barrier, inc=1, device_id={ctx_axis: me + hop}, device_id_type=MESH)

    pl.semaphore_wait(barrier, peers)

    def remote(src, dst, send, recv, to):
        return pltpu.make_async_remote_copy(
            src_ref=src, dst_ref=dst, send_sem=send, recv_sem=recv,
            device_id={ctx_axis: to}, device_id_type=MESH,
        )

    def halo_copy(way, to):
        first = rows - HALO if way == 0 else 0
        return remote(
            h_hbm.at[pl.ds(first, HALO), :], prev if way == 0 else follow,
            halo_send.at[way], halo_recv.at[way], to,
        )

    def decay_copy():
        return remote(dec.at[other], pair_dec, d_send, d_recv, partner)

    def pair_copy(g):
        return remote(state.at[other, g], pair_state.at[g], p_send.at[g], p_recv.at[g], partner)

    def chain_copy(g):
        return remote(send_buf.at[g], chain_in.at[g], c_send.at[g], c_recv.at[g], target)

    def hand_copy(d, g):
        return remote(chain_in.at[g], carry.at[d, g], f_send.at[g], f_recv.at[g], partner)

    @pl.when(me < n_ctx - 1)
    def _():
        halo_copy(0, me + 1).start()

    @pl.when(me > 0)
    def _():
        halo_copy(1, me - 1).start()

    gain = gain_ref[...].reshape(1, width)
    blocks = width // GROUP
    turn = anti(GROUP)

    def turned(ref):
        return jnp.concatenate(
            [dot(ref[:, (blocks - 1 - j) * GROUP : (blocks - j) * GROUP], turn) for j in range(blocks)], axis=1
        )

    def scale(u):
        return lax.rsqrt(jnp.mean(u * u, axis=1, keepdims=True) + epsilon)

    h_copy.wait()
    here = h_buf[...].astype(f32)
    factor = scale(here)
    n_buf[HALO:ext, :] = (here * factor * gain).astype(bf16)
    n_buf[ext : ext + rows, :] = (turned(h_buf) * factor * gain).astype(bf16)

    @pl.when(me > 0)
    def _():
        halo_copy(0, me - 1).wait_recv()

    @pl.when(me == 0)
    def _():
        prev[...] = jnp.zeros_like(prev)

    @pl.when(me < n_ctx - 1)
    def _():
        halo_copy(1, me + 1).wait_recv()

    @pl.when(me == n_ctx - 1)
    def _():
        follow[...] = jnp.zeros_like(follow)

    prior = prev[...].astype(f32)
    n_buf[0:HALO, :] = (prior * scale(prior) * gain).astype(bf16)
    later = turned(follow)
    n_buf[ext + rows :, :] = (later * scale(later) * gain).astype(bf16)

    bc_copy.wait()
    bc_in = dot(n_buf[...], bcw[...]).astype(bf16).astype(f32)
    bc[0] = conv_fwd(bc_in[:ext], bck_ref[...], rows)
    bc[1] = conv_bwd(bc_in[ext:], bck_ref[...], rows)
    raw = lax.dot_general(
        n_buf[HALO : ext + rows, :], dtw_ref[...], (((1,), (1,)), ((), ())), preferred_element_type=f32
    ) + dtb_ref[...]
    step = jnp.maximum(raw, 0.0) + jnp.log1p(jnp.exp(-jnp.abs(raw)))
    heads = raw.shape[1]
    pad[...] = jnp.zeros_like(pad)
    pad[0, :, 0:heads] = step
    pad[1, :, 0:heads] = -step * jnp.exp(rate_ref[...])
    ahead_rows = iota((rows, rows), 0) - iota((rows, rows), 1)
    for d in range(2):
        part = slice(d * rows, (d + 1) * rows)
        mask = ahead_rows >= 0 if d == 0 else ahead_rows <= 0
        total = dot(mask.astype(f32), pad[1, part, :], highest)
        end = total[rows - 1 : rows] if d == 0 else total[0:1]
        cumt[d] = total.T
        step_d = pad[0, part, :]
        delta[d] = pieces(step_d, 2)
        cum[d] = pieces(total, 3)
        wend[d] = pieces(jnp.exp(end - total) * step_d, 2)
        growth[d] = pieces(jnp.exp(total), 2)
        edge = total[half - 1 : half] if d == 0 else total[half : half + 1]
        low_part, high_part = total[:half], total[half:]
        if d == 0:
            mids = [jnp.exp(edge - low_part) * step_d[:half], jnp.exp(high_part - edge)]
        else:
            mids = [jnp.exp(low_part - edge), jnp.exp(edge - high_part) * step_d[half:]]
        mid[d] = pieces(jnp.concatenate(mids, axis=0), 2)
        last = pieces(jnp.broadcast_to(jnp.exp(end), (8, LANES)), 3)
        for g in range(groups):
            dec[d, g] = dot(last, spread(g, 3))
    decay_copy().start()

    def x_project(g):
        weight_copy(xw_hbm, xw, xw_sem, g).wait()
        x_in[g % 2] = dot(n_buf[...], xw[g]).astype(bf16)

    x_project(0)
    for g in range(groups):
        if g + 1 < groups:
            x_project(g + 1)
        now = x_in[g % 2].astype(f32)
        taps = xk_ref[:, g * GROUP : (g + 1) * GROUP]
        hot = spread(g)
        for d in range(2):
            x_conv = conv_fwd(now[:ext], taps, rows) if d == 0 else conv_bwd(now[ext:], taps, rows)
            x_buf[d, g] = x_conv
            weighted = (x_conv.astype(f32) * dot(wend[d], hot)).astype(bf16)
            state[d, g] = lax.dot_general(
                bc[d, :, :STATE], weighted, (((0,), (0,)), ((), ())), preferred_element_type=f32
            ).astype(bf16)
        pair_copy(g).start()

    for d in range(2):
        full = lax.dot_general(
            bc[d, :, STATE:], bc[d, :, :STATE], (((1,), (1,)), ((), ())), preferred_element_type=f32
        )
        gram[d] = jnp.where(ahead_rows >= 0 if d == 0 else ahead_rows <= 0, full, 0.0)

    def unit(g, _):
        weight_copy(zw_hbm, zw, zw_sem, g).wait()
        z_in = dot(n_buf[HALO : HALO + 2 * rows, :], zw[g]).astype(bf16)
        z_buf[g, 0] = z_in[:rows]
        z_buf[g, 1] = z_in[rows:]
        hot = spread(g)
        wide = spread(g, 3, half)
        per = GROUP // HEAD_DIM
        lane_head = iota((half, GROUP), 1) // HEAD_DIM
        for d in range(2):
            x_here = x_buf[d, g].astype(f32)
            scaled = x_here * dot(delta[d], hot)
            cols = dot(cum[d], wide)
            middle = dot(mid[d], hot)
            for b in range(2):
                here = slice(b * half, (b + 1) * half)
                there = slice((1 - b) * half, (2 - b) * half)
                parts, values = [], []
                for j in range(per):
                    column = cols[here, j * half : (j + 1) * half]
                    row = cumt[d, pl.ds(g * per + j, 1), :][:, here]
                    parts.append((jnp.exp(jnp.minimum(column - row, 0.0)) * gram[d, here, here]).astype(bf16))
                    values.append(jnp.where(lane_head == j, scaled[here], 0.0).astype(bf16))
                y = dot(jnp.concatenate(parts, axis=1), jnp.concatenate(values, axis=0))
                if b != d:
                    sent = (x_here[there] * middle[there]).astype(bf16)
                    y = y + middle[here] * dot(gram[d, here, there].astype(bf16), sent)
                y_buf[g, d, here] = y
        return 0

    def chain(g, _):
        pair_copy(g).wait_recv()

        @pl.when(has_source)
        def _():
            chain_copy(g).wait_recv()

        @pl.when(jnp.logical_not(has_source))
        def _():
            chain_in[g] = jnp.zeros_like(chain_in[g])

        joined = chain_in[g].astype(f32) * pair_dec[g, 0:1, :] + pair_state[g].astype(f32)
        carry[mine, g] = joined.astype(bf16)

        @pl.when(has_target)
        def _():
            send_buf[g] = (joined * dec[mine, g, 0:1, :] + state[mine, g].astype(f32)).astype(bf16)
            chain_copy(g).start()

        @pl.when(has_source)
        def _():
            hand_copy(mine, g).start()

        return 0

    late = jnp.where(mine == 0, me // 2, n_ctx // 2 - 1 - me // 2)
    before = jnp.minimum(groups, 2 * late)
    lax.fori_loop(0, before, unit, 0)
    decay_copy().wait_recv()
    lax.fori_loop(0, groups, chain, 0)
    lax.fori_loop(before, groups, unit, 0)

    same = iota((GROUP, GROUP), 0) // HEAD_DIM == iota((GROUP, GROUP), 1) // HEAD_DIM
    average = jnp.where(same, 1.0 / HEAD_DIM, 0.0).astype(bf16)
    out_gain[...] = out_gain_ref[...].reshape(1, groups * GROUP)

    def finish(d, g):
        carried = dot(bc[d, :, STATE:], carry[d, g]) * dot(growth[d], spread(g))
        value = (y_buf[g, d] + carried) * silu(z_buf[g, d].astype(f32))
        square = value * value
        high = square.astype(bf16)
        low = (square - high.astype(f32)).astype(bf16)
        mean_sq = dot(high, average) + dot(low, average)
        lanes = pl.ds(pl.multiple_of(g * GROUP, GROUP), GROUP)
        gated[d, :, lanes] = (value * lax.rsqrt(mean_sq + epsilon) * out_gain[:, lanes]).astype(bf16)

    def finish_mine(g, _):
        finish(mine, g)
        return 0

    def finish_other(g, _):
        @pl.when(other_source)
        def _():
            hand_copy(other, g).wait_recv()

        @pl.when(jnp.logical_not(other_source))
        def _():
            carry[other, g] = jnp.zeros_like(carry[other, g])

        finish(other, g)
        return 0

    lax.fori_loop(0, groups, finish_mine, 0)
    lax.fori_loop(0, groups, finish_other, 0)

    o_copy.wait()
    flip = anti(LANES)
    blocks = ow_hbm.shape[1] // block

    cuts = ((0, GROUP), (GROUP, block))

    def project(which, first, last):
        here = pl.multiple_of(which * block + first, LANES)
        there = pl.multiple_of((blocks - which) * block - last, LANES)
        ahead = dot(gated[0], ow[:, pl.ds(here, last - first)])
        back = dot(gated[1], ow[:, pl.ds(there, last - first)]).astype(bf16)
        count = (last - first) // LANES
        turned = [
            dot(back[:, (count - 1 - j) * LANES : (count - j) * LANES], flip) for j in range(count)
        ]
        return ahead + jnp.concatenate(turned, axis=1)

    def reduce_copy(src, dst, slot, cut, peer):
        lanes = pl.ds(cut[0], cut[1] - cut[0])
        return pltpu.make_async_remote_copy(
            src_ref=src.at[:, lanes],
            dst_ref=dst.at[:, lanes],
            send_sem=r_send.at[slot],
            recv_sem=r_recv.at[slot],
            device_id={head_axis: peer},
            device_id_type=MESH,
        )

    nears = [reduce_copy(one_send.at[0], one_recv.at[0], i, cut, sibling) for i, cut in enumerate(cuts)]
    fars = [reduce_copy(two_send, two_recv, 2 + i, cut, across) for i, cut in enumerate(cuts)]
    last_near = reduce_copy(one_send.at[1], one_recv.at[1], 4, (0, block), sibling)
    opposite = (1 - side) * 2 + (1 - core)

    def pass_on(i, partial):
        lanes = slice(*cuts[i])
        nears[i].wait_recv()
        two_send[:, lanes] = (partial + one_recv[0, :, lanes].astype(f32)).astype(bf16)
        fars[i].start()

    for i, cut in enumerate(cuts):
        one_send[0, :, cut[0] : cut[1]] = project(opposite, *cut).astype(bf16)
        nears[i].start()
        if i > 0:
            pass_on(i - 1, partial)
        partial = project(across, *cut)
    pass_on(len(cuts) - 1, partial)
    one_send[1] = project(sibling, 0, block).astype(bf16)
    last_near.start()
    partial = project(place, 0, block)
    residual = h_buf[:, pl.ds(pl.multiple_of(place * block, LANES), block)].astype(f32)
    last_near.wait_recv()
    partial = partial + one_recv[1].astype(f32)
    for i, cut in enumerate(cuts):
        lanes = slice(*cut)
        fars[i].wait_recv()
        summed = partial[:, lanes] + two_recv[:, lanes].astype(f32)
        out_ref[:, lanes] = (residual[:, lanes] + summed).astype(out_ref.dtype)
    for copy in (*nears, *fars, last_near):
        copy.wait_send()

    @pl.when(me < n_ctx - 1)
    def _():
        halo_copy(0, me + 1).wait_send()

    @pl.when(me > 0)
    def _():
        halo_copy(1, me - 1).wait_send()

    decay_copy().wait_send()

    def drain(g, _):
        pair_copy(g).wait_send()

        @pl.when(has_target)
        def _():
            chain_copy(g).wait_send()

        @pl.when(has_source)
        def _():
            hand_copy(mine, g).wait_send()

        return 0

    lax.fori_loop(0, groups, drain, 0)


def per_device(
    mesh,
    hidden,
    norm_gain,
    x_weight,
    z_weight,
    bc_weight,
    dt_weight,
    x_kernel,
    bc_kernel,
    dt_bias,
    log_rate,
    out_gain,
    out_weight,
):
    rows, width = hidden.shape
    inner = x_weight.shape[1]
    groups = inner // GROUP
    block = width // mesh.shape["head"]
    ext = rows + HALO
    vmem = pl.BlockSpec(memory_space=pltpu.VMEM)
    hbm = pl.BlockSpec(memory_space=pl.ANY)
    dma = pltpu.SemaphoreType.DMA
    return pl.pallas_call(
        functools.partial(kernel, mesh.shape["ctx"], ("ctx", "head")),
        out_shape=jax.ShapeDtypeStruct((rows, block), hidden.dtype),
        in_specs=[vmem] * 7 + [hbm] * 5,
        out_specs=vmem,
        scratch_shapes=[
            pltpu.VMEM((rows, width), bf16),
            pltpu.VMEM((HALO, width), bf16),
            pltpu.VMEM((HALO, width), bf16),
            pltpu.VMEM((width, 2 * STATE), bf16),
            pltpu.VMEM((groups, width, GROUP), bf16),
            pltpu.VMEM((groups, width, GROUP), bf16),
            pltpu.VMEM((inner, width), bf16),
            pltpu.VMEM((2 * ext, width), bf16),
            pltpu.VMEM((2, 2 * rows, LANES), f32),
            pltpu.VMEM((2, rows, 2 * STATE), bf16),
            pltpu.VMEM((2, rows, 2 * LANES), bf16),
            pltpu.VMEM((2, rows, 3 * LANES), bf16),
            pltpu.VMEM((2, LANES, rows), f32),
            pltpu.VMEM((2, rows, 2 * LANES), bf16),
            pltpu.VMEM((2, rows, 2 * LANES), bf16),
            pltpu.VMEM((2, rows, 2 * LANES), bf16),
            pltpu.VMEM((2, groups, 8, GROUP), f32),
            pltpu.VMEM((groups, 8, GROUP), f32),
            pltpu.VMEM((2, 2 * ext, GROUP), bf16),
            pltpu.VMEM((1, inner), f32),
            pltpu.VMEM((2, groups, rows, GROUP), bf16),
            pltpu.VMEM((groups, 2, rows, GROUP), bf16),
            pltpu.VMEM((groups, 2, rows, GROUP), f32),
            pltpu.VMEM((2, rows, inner), bf16),
            pltpu.VMEM((2, rows, rows), f32),
            pltpu.VMEM((2, groups, STATE, GROUP), bf16),
            pltpu.VMEM((groups, STATE, GROUP), bf16),
            pltpu.VMEM((groups, STATE, GROUP), bf16),
            pltpu.VMEM((2, groups, STATE, GROUP), bf16),
            pltpu.VMEM((groups, STATE, GROUP), bf16),
            pltpu.VMEM((2, rows, block), bf16),
            pltpu.VMEM((2, rows, block), bf16),
            pltpu.VMEM((rows, block), bf16),
            pltpu.VMEM((rows, block), bf16),
            dma((3,)),
            dma((groups,)),
            dma((groups,)),
            dma((2,)),
            dma((2,)),
            dma,
            dma,
            dma((groups,)),
            dma((groups,)),
            dma((groups,)),
            dma((groups,)),
            dma((groups,)),
            dma((groups,)),
            dma((5,)),
            dma((5,)),
        ],
        compiler_params=pltpu.CompilerParams(
            collective_id=0, has_side_effects=True, vmem_limit_bytes=60 * 2**20
        ),
        cost_estimate=pl.CostEstimate(flops=12_000_000_000, bytes_accessed=24_000_000, transcendentals=5_000_000),
        name="mixer",
    )(
        norm_gain,
        dt_weight.T,
        x_kernel,
        bc_kernel,
        dt_bias[None],
        log_rate[None],
        out_gain,
        hidden,
        x_weight,
        z_weight,
        bc_weight,
        out_weight,
    )


def solution(mesh):
    return jax.shard_map(
        functools.partial(per_device, mesh),
        mesh=mesh,
        in_specs=(
            P("ctx", None),
            P(),
            P(None, "head"),
            P(None, "head"),
            P(),
            P(None, "head"),
            P(None, "head"),
            P(),
            P("head"),
            P("head"),
            P("head"),
            P("head", None),
        ),
        out_specs=P("ctx", "head"),
        check_vma=False,
    )
```

```python
import functools

import jax
import jax.numpy as jnp
from jax import lax
from jax.experimental import pallas as pl
from jax.experimental.pallas import tpu as pltpu
from jax.sharding import PartitionSpec as P

HEAD_DIM = 64
STATE = 128
GROUP = 256
LANES = 128
HALO = 16
epsilon = 1e-05
highest = lax.Precision.HIGHEST
MESH = pl.DeviceIdType.MESH
f32 = jnp.float32
bf16 = jnp.bfloat16


def iota(shape, dim):
    return lax.broadcasted_iota(jnp.int32, shape, dim)


def dot(a, b, precision=None):
    return jnp.dot(a, b, preferred_element_type=f32, precision=precision)


def silu(v):
    half = 0.5 * v
    return half + half * jnp.tanh(half)


def pieces(v, count):
    out = []
    for _ in range(count):
        part = v.astype(bf16)
        out.append(part)
        v = v - part.astype(f32)
    return jnp.concatenate(out, axis=1)


def anti(size):
    return (iota((size, size), 0) + iota((size, size), 1) == size - 1).astype(bf16)


def spread(group, count=2, each=HEAD_DIM):
    per = GROUP // HEAD_DIM
    shape = (count * LANES, per * each)
    head = group * per + iota(shape, 1) // each
    return (lax.rem(iota(shape, 0), LANES) == head).astype(bf16)


def conv_fwd(ext, taps, rows):
    out = taps[0:1] * ext[HALO - 3 : HALO - 3 + rows]
    for k in range(1, 4):
        out = out + taps[k : k + 1] * ext[HALO - 3 + k : HALO - 3 + k + rows]
    return silu(out).astype(bf16)


def conv_bwd(ext, taps, rows):
    out = taps[0:1] * ext[3 : 3 + rows]
    for k in range(1, 4):
        out = out + taps[k : k + 1] * ext[3 - k : 3 - k + rows]
    return silu(out).astype(bf16)


def kernel(
    n_ctx, axes,
    gain_ref, dtw_ref, xk_ref, bck_ref, dtb_ref, rate_ref, out_gain_ref, h_hbm, xw_hbm, zw_hbm, bcw_hbm, ow_hbm,
    out_ref,
    h_buf, prev, follow, bcw, xw, zw, ow, n_buf, pad, bc, delta, cum, cumt, wend, growth, mid, dec, pair_dec, x_in, out_gain,
    x_buf, z_buf, y_buf, gated, gram, state, pair_state, chain_in, carry, send_buf,
    one_send, one_recv, two_send, two_recv,
    in_sem, xw_sem, zw_sem, halo_send, halo_recv, d_send, d_recv, p_send, p_recv, c_send, c_recv, f_send, f_recv,
    r_send, r_recv,
):
    ctx_axis, head_axis = axes
    me = lax.axis_index(ctx_axis)
    place = lax.axis_index(head_axis)
    rows, width = h_buf.shape
    groups = x_buf.shape[1]
    block = out_ref.shape[1]
    ext = rows + HALO
    half = rows // 2
    core = lax.rem(place, 2)
    side = place // 2
    sibling = side * 2 + (1 - core)
    across = (1 - side) * 2 + core
    other = lax.rem(me, 2)
    mine = 1 - other
    partner = me + 1 - 2 * other
    target = me + 2 - 4 * mine
    source = me - 2 + 4 * mine
    has_source = jnp.logical_and(source >= 0, source < n_ctx)
    has_target = jnp.logical_and(target >= 0, target < n_ctx)
    their_source = partner - 2 + 4 * other
    other_source = jnp.logical_and(their_source >= 0, their_source < n_ctx)

    def weight_copy(hbm, buf, sem, g):
        lanes = pl.ds(pl.multiple_of(g * GROUP, GROUP), GROUP)
        return pltpu.make_async_copy(hbm.at[:, lanes], buf.at[g], sem.at[g])

    h_copy = pltpu.make_async_copy(h_hbm, h_buf, in_sem.at[0])
    bc_copy = pltpu.make_async_copy(bcw_hbm, bcw, in_sem.at[1])
    o_copy = pltpu.make_async_copy(ow_hbm, ow, in_sem.at[2])
    h_copy.start()
    bc_copy.start()
    for g in range(groups):
        weight_copy(xw_hbm, xw, xw_sem, g).start()
    for g in range(groups):
        weight_copy(zw_hbm, zw, zw_sem, g).start()
    o_copy.start()

    barrier = pltpu.get_barrier_semaphore()
    for peer in (sibling, across):
        pl.semaphore_signal(barrier, inc=1, device_id={head_axis: peer}, device_id_type=MESH)
    peers = 2
    for hop in (-2, -1, 1, 2):
        present = jnp.logical_and(me + hop >= 0, me + hop < n_ctx)
        peers = peers + jnp.where(present, 1, 0)

        @pl.when(present)
        def _():
            pl.semaphore_signal(barrier, inc=1, device_id={ctx_axis: me + hop}, device_id_type=MESH)

    pl.semaphore_wait(barrier, peers)

    def remote(src, dst, send, recv, to):
        return pltpu.make_async_remote_copy(
            src_ref=src, dst_ref=dst, send_sem=send, recv_sem=recv,
            device_id={ctx_axis: to}, device_id_type=MESH,
        )

    def halo_copy(way, to):
        first = rows - HALO if way == 0 else 0
        return remote(
            h_hbm.at[pl.ds(first, HALO), :], prev if way == 0 else follow,
            halo_send.at[way], halo_recv.at[way], to,
        )

    def decay_copy():
        return remote(dec.at[other], pair_dec, d_send, d_recv, partner)

    def pair_copy(g):
        return remote(state.at[other, g], pair_state.at[g], p_send.at[g], p_recv.at[g], partner)

    def chain_copy(g):
        return remote(send_buf.at[g], chain_in.at[g], c_send.at[g], c_recv.at[g], target)

    def hand_copy(d, g):
        return remote(chain_in.at[g], carry.at[d, g], f_send.at[g], f_recv.at[g], partner)

    @pl.when(me < n_ctx - 1)
    def _():
        halo_copy(0, me + 1).start()

    @pl.when(me > 0)
    def _():
        halo_copy(1, me - 1).start()

    gain = gain_ref[...].reshape(1, width)
    blocks = width // GROUP
    turn = anti(GROUP)

    def turned(ref):
        return jnp.concatenate(
            [dot(ref[:, (blocks - 1 - j) * GROUP : (blocks - j) * GROUP], turn) for j in range(blocks)], axis=1
        )

    def scale(u):
        return lax.rsqrt(jnp.mean(u * u, axis=1, keepdims=True) + epsilon)

    h_copy.wait()
    here = h_buf[...].astype(f32)
    factor = scale(here)
    n_buf[HALO:ext, :] = (here * factor * gain).astype(bf16)
    n_buf[ext : ext + rows, :] = (turned(h_buf) * factor * gain).astype(bf16)

    @pl.when(me > 0)
    def _():
        halo_copy(0, me - 1).wait_recv()

    @pl.when(me == 0)
    def _():
        prev[...] = jnp.zeros_like(prev)

    @pl.when(me < n_ctx - 1)
    def _():
        halo_copy(1, me + 1).wait_recv()

    @pl.when(me == n_ctx - 1)
    def _():
        follow[...] = jnp.zeros_like(follow)

    prior = prev[...].astype(f32)
    n_buf[0:HALO, :] = (prior * scale(prior) * gain).astype(bf16)
    later = turned(follow)
    n_buf[ext + rows :, :] = (later * scale(later) * gain).astype(bf16)

    bc_copy.wait()
    bc_in = dot(n_buf[...], bcw[...]).astype(bf16).astype(f32)
    bc[0] = conv_fwd(bc_in[:ext], bck_ref[...], rows)
    bc[1] = conv_bwd(bc_in[ext:], bck_ref[...], rows)
    raw = lax.dot_general(
        n_buf[HALO : ext + rows, :], dtw_ref[...], (((1,), (1,)), ((), ())), preferred_element_type=f32
    ) + dtb_ref[...]
    step = jnp.maximum(raw, 0.0) + jnp.log1p(jnp.exp(-jnp.abs(raw)))
    heads = raw.shape[1]
    pad[...] = jnp.zeros_like(pad)
    pad[0, :, 0:heads] = step
    pad[1, :, 0:heads] = -step * jnp.exp(rate_ref[...])
    ahead_rows = iota((rows, rows), 0) - iota((rows, rows), 1)
    for d in range(2):
        part = slice(d * rows, (d + 1) * rows)
        mask = ahead_rows >= 0 if d == 0 else ahead_rows <= 0
        total = dot(mask.astype(f32), pad[1, part, :], highest)
        end = total[rows - 1 : rows] if d == 0 else total[0:1]
        cumt[d] = total.T
        step_d = pad[0, part, :]
        delta[d] = pieces(step_d, 2)
        cum[d] = pieces(total, 3)
        wend[d] = pieces(jnp.exp(end - total) * step_d, 2)
        growth[d] = pieces(jnp.exp(total), 2)
        edge = total[half - 1 : half] if d == 0 else total[half : half + 1]
        low_part, high_part = total[:half], total[half:]
        if d == 0:
            mids = [jnp.exp(edge - low_part) * step_d[:half], jnp.exp(high_part - edge)]
        else:
            mids = [jnp.exp(low_part - edge), jnp.exp(edge - high_part) * step_d[half:]]
        mid[d] = pieces(jnp.concatenate(mids, axis=0), 2)
        last = pieces(jnp.broadcast_to(jnp.exp(end), (8, LANES)), 3)
        for g in range(groups):
            dec[d, g] = dot(last, spread(g, 3))
    decay_copy().start()

    def x_project(g):
        weight_copy(xw_hbm, xw, xw_sem, g).wait()
        x_in[g % 2] = dot(n_buf[...], xw[g]).astype(bf16)

    x_project(0)
    for g in range(groups):
        if g + 1 < groups:
            x_project(g + 1)
        now = x_in[g % 2].astype(f32)
        taps = xk_ref[:, g * GROUP : (g + 1) * GROUP]
        hot = spread(g)
        for d in range(2):
            x_conv = conv_fwd(now[:ext], taps, rows) if d == 0 else conv_bwd(now[ext:], taps, rows)
            x_buf[d, g] = x_conv
            weighted = (x_conv.astype(f32) * dot(wend[d], hot)).astype(bf16)
            state[d, g] = lax.dot_general(
                bc[d, :, :STATE], weighted, (((0,), (0,)), ((), ())), preferred_element_type=f32
            ).astype(bf16)
        pair_copy(g).start()

    for d in range(2):
        full = lax.dot_general(
            bc[d, :, STATE:], bc[d, :, :STATE], (((1,), (1,)), ((), ())), preferred_element_type=f32
        )
        gram[d] = jnp.where(ahead_rows >= 0 if d == 0 else ahead_rows <= 0, full, 0.0)

    def unit(g, _):
        weight_copy(zw_hbm, zw, zw_sem, g).wait()
        z_in = dot(n_buf[HALO : HALO + 2 * rows, :], zw[g]).astype(bf16)
        z_buf[g, 0] = z_in[:rows]
        z_buf[g, 1] = z_in[rows:]
        hot = spread(g)
        wide = spread(g, 3, half)
        per = GROUP // HEAD_DIM
        lane_head = iota((half, GROUP), 1) // HEAD_DIM
        for d in range(2):
            x_here = x_buf[d, g].astype(f32)
            scaled = x_here * dot(delta[d], hot)
            cols = dot(cum[d], wide)
            middle = dot(mid[d], hot)
            for b in range(2):
                here = slice(b * half, (b + 1) * half)
                there = slice((1 - b) * half, (2 - b) * half)
                parts, values = [], []
                for j in range(per):
                    column = cols[here, j * half : (j + 1) * half]
                    row = cumt[d, pl.ds(g * per + j, 1), :][:, here]
                    parts.append((jnp.exp(jnp.minimum(column - row, 0.0)) * gram[d, here, here]).astype(bf16))
                    values.append(jnp.where(lane_head == j, scaled[here], 0.0).astype(bf16))
                y = dot(jnp.concatenate(parts, axis=1), jnp.concatenate(values, axis=0))
                if b != d:
                    sent = (x_here[there] * middle[there]).astype(bf16)
                    y = y + middle[here] * dot(gram[d, here, there].astype(bf16), sent)
                y_buf[g, d, here] = y
        return 0

    def chain(g, _):
        pair_copy(g).wait_recv()

        @pl.when(has_source)
        def _():
            chain_copy(g).wait_recv()

        @pl.when(jnp.logical_not(has_source))
        def _():
            chain_in[g] = jnp.zeros_like(chain_in[g])

        joined = chain_in[g].astype(f32) * pair_dec[g, 0:1, :] + pair_state[g].astype(f32)
        carry[mine, g] = joined.astype(bf16)

        @pl.when(has_target)
        def _():
            send_buf[g] = (joined * dec[mine, g, 0:1, :] + state[mine, g].astype(f32)).astype(bf16)
            chain_copy(g).start()

        @pl.when(has_source)
        def _():
            hand_copy(mine, g).start()

        return 0

    late = jnp.where(mine == 0, me // 2, n_ctx // 2 - 1 - me // 2)
    before = jnp.minimum(groups, 2 * late)
    same = iota((GROUP, GROUP), 0) // HEAD_DIM == iota((GROUP, GROUP), 1) // HEAD_DIM
    average = jnp.where(same, 1.0 / HEAD_DIM, 0.0).astype(bf16)
    out_gain[...] = out_gain_ref[...].reshape(1, groups * GROUP)

    def finish(d, g):
        carried = dot(bc[d, :, STATE:], carry[d, g]) * dot(growth[d], spread(g))
        value = (y_buf[g, d] + carried) * silu(z_buf[g, d].astype(f32))
        square = value * value
        high = square.astype(bf16)
        low = (square - high.astype(f32)).astype(bf16)
        mean_sq = dot(high, average) + dot(low, average)
        lanes = pl.ds(pl.multiple_of(g * GROUP, GROUP), GROUP)
        gated[d, :, lanes] = (value * lax.rsqrt(mean_sq + epsilon) * out_gain[:, lanes]).astype(bf16)

    def finish_mine(g, _):
        finish(mine, g)
        return 0

    def finish_other(g, _):
        @pl.when(other_source)
        def _():
            hand_copy(other, g).wait_recv()

        @pl.when(jnp.logical_not(other_source))
        def _():
            carry[other, g] = jnp.zeros_like(carry[other, g])

        finish(other, g)
        return 0

    done = before >= groups
    early = jnp.logical_and(done, jnp.logical_not(other_source))

    def link(g, _):
        chain(g, 0)

        @pl.when(done)
        def _():
            finish(mine, g)

        @pl.when(early)
        def _():
            finish_other(g, 0)

        return 0

    lax.fori_loop(0, before, unit, 0)
    decay_copy().wait_recv()
    lax.fori_loop(0, groups, link, 0)
    lax.fori_loop(before, groups, unit, 0)
    lax.fori_loop(0, jnp.where(done, 0, groups), finish_mine, 0)
    lax.fori_loop(0, jnp.where(early, 0, groups), finish_other, 0)

    o_copy.wait()
    flip = anti(LANES)
    blocks = ow_hbm.shape[1] // block

    cuts = ((0, GROUP), (GROUP, block))

    def project(which, first, last):
        here = pl.multiple_of(which * block + first, LANES)
        there = pl.multiple_of((blocks - which) * block - last, LANES)
        ahead = dot(gated[0], ow[:, pl.ds(here, last - first)])
        back = dot(gated[1], ow[:, pl.ds(there, last - first)]).astype(bf16)
        count = (last - first) // LANES
        turned = [
            dot(back[:, (count - 1 - j) * LANES : (count - j) * LANES], flip) for j in range(count)
        ]
        return ahead + jnp.concatenate(turned, axis=1)

    def reduce_copy(src, dst, slot, cut, peer):
        lanes = pl.ds(cut[0], cut[1] - cut[0])
        return pltpu.make_async_remote_copy(
            src_ref=src.at[:, lanes],
            dst_ref=dst.at[:, lanes],
            send_sem=r_send.at[slot],
            recv_sem=r_recv.at[slot],
            device_id={head_axis: peer},
            device_id_type=MESH,
        )

    nears = [reduce_copy(one_send.at[0], one_recv.at[0], i, cut, sibling) for i, cut in enumerate(cuts)]
    fars = [reduce_copy(two_send, two_recv, 2 + i, cut, across) for i, cut in enumerate(cuts)]
    last_near = reduce_copy(one_send.at[1], one_recv.at[1], 4, (0, block), sibling)
    opposite = (1 - side) * 2 + (1 - core)

    def pass_on(i, partial):
        lanes = slice(*cuts[i])
        nears[i].wait_recv()
        two_send[:, lanes] = (partial + one_recv[0, :, lanes].astype(f32)).astype(bf16)
        fars[i].start()

    for i, cut in enumerate(cuts):
        one_send[0, :, cut[0] : cut[1]] = project(opposite, *cut).astype(bf16)
        nears[i].start()
        if i > 0:
            pass_on(i - 1, partial)
        partial = project(across, *cut)
    pass_on(len(cuts) - 1, partial)
    one_send[1] = project(sibling, 0, block).astype(bf16)
    last_near.start()
    partial = project(place, 0, block)
    residual = h_buf[:, pl.ds(pl.multiple_of(place * block, LANES), block)].astype(f32)
    last_near.wait_recv()
    partial = partial + one_recv[1].astype(f32)
    for i, cut in enumerate(cuts):
        lanes = slice(*cut)
        fars[i].wait_recv()
        summed = partial[:, lanes] + two_recv[:, lanes].astype(f32)
        out_ref[:, lanes] = (residual[:, lanes] + summed).astype(out_ref.dtype)
    for copy in (*nears, *fars, last_near):
        copy.wait_send()

    @pl.when(me < n_ctx - 1)
    def _():
        halo_copy(0, me + 1).wait_send()

    @pl.when(me > 0)
    def _():
        halo_copy(1, me - 1).wait_send()

    decay_copy().wait_send()

    def drain(g, _):
        pair_copy(g).wait_send()

        @pl.when(has_target)
        def _():
            chain_copy(g).wait_send()

        @pl.when(has_source)
        def _():
            hand_copy(mine, g).wait_send()

        return 0

    lax.fori_loop(0, groups, drain, 0)


def per_device(
    mesh,
    hidden,
    norm_gain,
    x_weight,
    z_weight,
    bc_weight,
    dt_weight,
    x_kernel,
    bc_kernel,
    dt_bias,
    log_rate,
    out_gain,
    out_weight,
):
    rows, width = hidden.shape
    inner = x_weight.shape[1]
    groups = inner // GROUP
    block = width // mesh.shape["head"]
    ext = rows + HALO
    vmem = pl.BlockSpec(memory_space=pltpu.VMEM)
    hbm = pl.BlockSpec(memory_space=pl.ANY)
    dma = pltpu.SemaphoreType.DMA
    return pl.pallas_call(
        functools.partial(kernel, mesh.shape["ctx"], ("ctx", "head")),
        out_shape=jax.ShapeDtypeStruct((rows, block), hidden.dtype),
        in_specs=[vmem] * 7 + [hbm] * 5,
        out_specs=vmem,
        scratch_shapes=[
            pltpu.VMEM((rows, width), bf16),
            pltpu.VMEM((HALO, width), bf16),
            pltpu.VMEM((HALO, width), bf16),
            pltpu.VMEM((width, 2 * STATE), bf16),
            pltpu.VMEM((groups, width, GROUP), bf16),
            pltpu.VMEM((groups, width, GROUP), bf16),
            pltpu.VMEM((inner, width), bf16),
            pltpu.VMEM((2 * ext, width), bf16),
            pltpu.VMEM((2, 2 * rows, LANES), f32),
            pltpu.VMEM((2, rows, 2 * STATE), bf16),
            pltpu.VMEM((2, rows, 2 * LANES), bf16),
            pltpu.VMEM((2, rows, 3 * LANES), bf16),
            pltpu.VMEM((2, LANES, rows), f32),
            pltpu.VMEM((2, rows, 2 * LANES), bf16),
            pltpu.VMEM((2, rows, 2 * LANES), bf16),
            pltpu.VMEM((2, rows, 2 * LANES), bf16),
            pltpu.VMEM((2, groups, 8, GROUP), f32),
            pltpu.VMEM((groups, 8, GROUP), f32),
            pltpu.VMEM((2, 2 * ext, GROUP), bf16),
            pltpu.VMEM((1, inner), f32),
            pltpu.VMEM((2, groups, rows, GROUP), bf16),
            pltpu.VMEM((groups, 2, rows, GROUP), bf16),
            pltpu.VMEM((groups, 2, rows, GROUP), f32),
            pltpu.VMEM((2, rows, inner), bf16),
            pltpu.VMEM((2, rows, rows), f32),
            pltpu.VMEM((2, groups, STATE, GROUP), bf16),
            pltpu.VMEM((groups, STATE, GROUP), bf16),
            pltpu.VMEM((groups, STATE, GROUP), bf16),
            pltpu.VMEM((2, groups, STATE, GROUP), bf16),
            pltpu.VMEM((groups, STATE, GROUP), bf16),
            pltpu.VMEM((2, rows, block), bf16),
            pltpu.VMEM((2, rows, block), bf16),
            pltpu.VMEM((rows, block), bf16),
            pltpu.VMEM((rows, block), bf16),
            dma((3,)),
            dma((groups,)),
            dma((groups,)),
            dma((2,)),
            dma((2,)),
            dma,
            dma,
            dma((groups,)),
            dma((groups,)),
            dma((groups,)),
            dma((groups,)),
            dma((groups,)),
            dma((groups,)),
            dma((5,)),
            dma((5,)),
        ],
        compiler_params=pltpu.CompilerParams(
            collective_id=0, has_side_effects=True, vmem_limit_bytes=60 * 2**20
        ),
        cost_estimate=pl.CostEstimate(flops=12_000_000_000, bytes_accessed=24_000_000, transcendentals=5_000_000),
        name="mixer",
    )(
        norm_gain,
        dt_weight.T,
        x_kernel,
        bc_kernel,
        dt_bias[None],
        log_rate[None],
        out_gain,
        hidden,
        x_weight,
        z_weight,
        bc_weight,
        out_weight,
    )


def solution(mesh):
    return jax.shard_map(
        functools.partial(per_device, mesh),
        mesh=mesh,
        in_specs=(
            P("ctx", None),
            P(),
            P(None, "head"),
            P(None, "head"),
            P(),
            P(None, "head"),
            P(None, "head"),
            P(),
            P("head"),
            P("head"),
            P("head"),
            P("head", None),
        ),
        out_specs=P("ctx", "head"),
        check_vma=False,
    )
```
